128 devices in a mesh: wide: 16 (over z_lo, x, core), narrow: 8 (over z_hi, y).
Axes of the slice: x: 4, y: 4, z: 4 (z_hi: 2, z_lo: 2; z = z_hi * 2 + z_lo), core: 2. Of those that a mesh axis runs over, the one named last changes fastest.
Arguments:
- velocity: float32 [3, 128, 64, 128], P(None, 'wide', 'narrow'), may hold values from -6 to 6
- force: float32 [3, 128, 64, 128], P(None, 'wide', 'narrow'), may hold values from -6 to 6
- visc_class: int32 [128, 64, 128], P('wide', 'narrow'), may hold values from 0 to 3
- visc_table: float32 [4], replicated, may hold values from 0.2 to 5
- multiplier: float32 [3, 256, 2048], P(None, ('wide', 'narrow')), may hold values from -6 to 6
- marker_cell: int32 [256, 2048], P(('wide', 'narrow')), may hold values from 0 to 8190, as said below
- marker_frac: float32 [3, 256, 2048], P(None, ('wide', 'narrow')), may hold values from 0 to 1
- pair_sphere: int32 [4096], P(('wide', 'narrow')), may hold values from 0 to 1
- pair_partner: int32 [4096], P(('wide', 'narrow')), may hold values from 0 to 17
- pair_normal: float32 [3, 4096], P(None, ('wide', 'narrow')), may hold values from -6 to 6
- pair_gap: float32 [4096], P(('wide', 'narrow')), may hold values from -6 to 6
- contact_force: float32 [4096], P(('wide', 'narrow')), may hold values from 0 to 1
Outputs:
- fluid_velocity: float32 [3, 128, 64, 128], P(None, 'wide', 'narrow')
- rigid_multiplier: float32 [3, 256, 2048], P(None, ('wide', 'narrow'))
- contact_multiplier: float32 [4096], P(('wide', 'narrow'))
The draws below stay inside these ranges and needn't reach their ends.
Inputs may be any that keep to these rules, and one draw needn't show every extreme that they name: marker_cell[s, m] = (i * 8 + j) * 128 + k for a cell (i, j, k) of the brick that owns sphere s, with k <= 126; the markers of one sphere lie within a few cells of each other.
All inputs are finite; a program needn't handle non-finite values.
Results may differ from the reference program's by a relative error of at most 0.0003.
Values sent between devices are 32-bit elements; how exact they have to be, the bound alone decides.
A program may use at most 64 MiB of HBM per device.

```python
import math
import jax
import jax.numpy as jnp

CX = 8
CY = 8
NZ = 128
SPH_DEV = 2
MARK = 2048
PAIRS_DEV = 32
NVISC = 4
ITERS = 2
SWEEPS = 2
NX = 128
NY = 64
SPHERES = 256
PAIRS = 4096
N_WIDE = 16
N_NARROW = 8


def draw_marker_cell(key, part):
    keys = jax.random.split(jax.random.fold_in(key, 11), 6)
    centre_x = jax.random.randint(keys[0], (SPHERES, 1), 0, CX)
    centre_y = jax.random.randint(keys[1], (SPHERES, 1), 0, CY)
    centre_z = jax.random.randint(keys[2], (SPHERES, 1), 0, NZ - 1)
    cell_x = jnp.clip(centre_x + jax.random.randint(keys[3], (SPHERES, MARK), -4, 5), 0, CX - 1)
    cell_y = jnp.clip(centre_y + jax.random.randint(keys[4], (SPHERES, MARK), -4, 5), 0, CY - 1)
    cell_z = jnp.clip(centre_z + jax.random.randint(keys[5], (SPHERES, MARK), -4, 5), 0, NZ - 2)
    result = (cell_x * CY + cell_y) * NZ + cell_z
    result = result.at[0, 0].set(0)
    result = result.at[0, 1].set(CX * CY * NZ - 2)
    return result.astype(jnp.int32)


def set_ends(values, own_key, least, top_value):
    longest = values.shape.index(max(values.shape))
    spots = []
    for shift in (0, 1):
        where = [jax.random.randint(jax.random.fold_in(own_key, axis), (), 0, length) for axis, length in enumerate(values.shape)]
        where[longest] = (where[longest] + shift) % values.shape[longest]
        spots.append(tuple(where))
    return values.at[spots[0]].set(least).at[spots[1]].set(top_value)


def block_levels(own_key, dims, cuts, least, high):
    def one(position, shards_of):
        steps = jax.random.uniform(jax.random.fold_in(jax.random.fold_in(own_key, 6), position), (shards_of,), jnp.float32, least / len(cuts), high / len(cuts))
        return jnp.repeat(jnp.exp(steps), dims[position] // shards_of).reshape((-1,) + (1,) * (len(dims) - position - 1))

    level = one(*cuts[0])
    for cut in cuts[1:]:
        level = level * one(*cut)
    return level


def bell_draw(key, extent, spread, limit, cuts=(), kind=jnp.bfloat16):
    loudness = block_levels(key, extent, cuts, -0.22, 0.18) if cuts else 1.0
    array = jax.random.normal(key, extent, jnp.float32) * spread * loudness
    return jnp.minimum(jnp.maximum(array, -limit), limit).astype(kind)


def setup_inputs(seed: int = 0) -> dict:
    key_of = jax.random.split(jax.random.key(seed), 13)
    velocity = bell_draw(key_of[0], (3, NX, NY, NZ), 1.0, 6.0, ((1, 16), (2, 8)), jnp.float32)
    force = bell_draw(key_of[1], (3, NX, NY, NZ), 1.0, 6.0, ((1, 16), (2, 8)), jnp.float32)
    visc_class = set_ends(jax.random.randint(key_of[2], (NX, NY, NZ), 0, NVISC), jax.random.fold_in(key_of[2], 1), 0, NVISC - 1).astype(jnp.int32)
    visc_table = jnp.clip(jnp.exp(jax.random.uniform(key_of[3], (NVISC,), jnp.float32, math.log(0.2), math.log(5.0))), 0.2, 5.0)
    multiplier = bell_draw(key_of[4], (3, SPHERES, MARK), 1.0, 6.0, ((1, 128),), jnp.float32)
    marker_cell = draw_marker_cell(jax.random.fold_in(key_of[12], 71), 0)
    marker_frac = jnp.clip(1.0 * jax.random.uniform(key_of[6], (3, SPHERES, MARK), jnp.float32) ** block_levels(key_of[6], (3, SPHERES, MARK), ((1, 128),), -0.2, 0.2), 0.0, 1.0)
    pair_sphere = set_ends(jax.random.randint(key_of[7], (PAIRS,), 0, SPH_DEV), jax.random.fold_in(key_of[7], 1), 0, SPH_DEV - 1).astype(jnp.int32)
    pair_partner = set_ends(jax.random.randint(key_of[8], (PAIRS,), 0, 9 * SPH_DEV), jax.random.fold_in(key_of[8], 1), 0, (9 * SPH_DEV) - 1).astype(jnp.int32)
    pair_normal = bell_draw(key_of[9], (3, PAIRS), 1.0, 6.0, ((1, 128),), jnp.float32)
    pair_gap = bell_draw(key_of[10], (PAIRS,), 1.0, 6.0, ((0, 128),), jnp.float32)
    contact_force = jnp.clip(1.0 * jax.random.uniform(key_of[11], (PAIRS,), jnp.float32) ** block_levels(key_of[11], (PAIRS,), ((0, 128),), -0.2, 0.2), 0.0, 1.0)
    return {"velocity": velocity, "force": force, "visc_class": visc_class, "visc_table": visc_table, "multiplier": multiplier, "marker_cell": marker_cell, "marker_frac": marker_frac, "pair_sphere": pair_sphere, "pair_partner": pair_partner, "pair_normal": pair_normal, "pair_gap": pair_gap, "contact_force": contact_force}


base_diag = 1.0
spread_gain = 0.25
rigid_step = 0.5
contact_step = 0.5
contact_gain = 0.5


def reference(velocity, force, visc_class, visc_table, multiplier, marker_cell, marker_frac, pair_sphere, pair_partner, pair_normal, pair_gap, contact_force):
    classes = jnp.arange(NVISC, dtype=jnp.int32)
    viscosity = jnp.sum(jnp.where(visc_class[None] == classes[:, None, None, None], visc_table[:, None, None, None], jnp.float32(0.0)), axis=0)
    padded_mu = jnp.pad(viscosity, 1)
    face_coef = [
        0.5 * (viscosity + padded_mu[:-2, 1:-1, 1:-1]),
        0.5 * (viscosity + padded_mu[2:, 1:-1, 1:-1]),
        0.5 * (viscosity + padded_mu[1:-1, :-2, 1:-1]),
        0.5 * (viscosity + padded_mu[1:-1, 2:, 1:-1]),
        0.5 * (viscosity + padded_mu[1:-1, 1:-1, :-2]),
        0.5 * (viscosity + padded_mu[1:-1, 1:-1, 2:]),
    ]
    diagonal = base_diag + face_coef[0] + face_coef[1] + face_coef[2] + face_coef[3] + face_coef[4] + face_coef[5]

    owner = jnp.arange(SPHERES, dtype=jnp.int32) // SPH_DEV
    column = owner // N_NARROW
    row = owner % N_NARROW
    cell_x = marker_cell // (CY * NZ) + column[:, None] * CX
    cell_y = (marker_cell // NZ) % CY + row[:, None] * CY
    cell_z = marker_cell % NZ
    corner_list = []
    for step_x in (0, 1):
        for step_y in (0, 1):
            for step_z in (0, 1):
                index = ((cell_x + step_x) * (NY + 1) + cell_y + step_y) * NZ + cell_z + step_z
                weight_x = marker_frac[0] if step_x else 1.0 - marker_frac[0]
                weight_y = marker_frac[1] if step_y else 1.0 - marker_frac[1]
                weight_z = marker_frac[2] if step_z else 1.0 - marker_frac[2]
                corner_list.append((index.reshape(-1).astype(jnp.int32), (weight_x * weight_y * weight_z).reshape(-1)))

    pair_owner = jnp.arange(PAIRS, dtype=jnp.int32) // PAIRS_DEV
    pair_column = pair_owner // N_NARROW
    pair_row = pair_owner % N_NARROW
    own_index = pair_owner * SPH_DEV + pair_sphere
    block = pair_partner // SPH_DEV
    target_column = pair_column + block // 3 - 1
    target_row = pair_row + block % 3 - 1
    valid = (target_column >= 0) & (target_column < N_WIDE) & (target_row >= 0) & (target_row < N_NARROW)
    partner_index = (jnp.clip(target_column, 0, N_WIDE - 1) * N_NARROW + jnp.clip(target_row, 0, N_NARROW - 1)) * SPH_DEV + pair_partner % SPH_DEV

    for outer in range(ITERS):
        flat_mult = multiplier.reshape(3, -1)
        grid = jnp.zeros((3, (NX + 1) * (NY + 1) * NZ), jnp.float32)
        for index, weight in corner_list:
            grid = grid.at[:, index].add(spread_gain * flat_mult * weight[None])
        grid_force = grid.reshape(3, NX + 1, NY + 1, NZ)[:, :NX, :NY]
        rhs = force + grid_force
        for inner in range(SWEEPS):
            grown = jnp.pad(velocity, ((0, 0), (1, 1), (1, 1), (1, 1)))
            neighbour_sum = (face_coef[0] * grown[:, :-2, 1:-1, 1:-1] + face_coef[1] * grown[:, 2:, 1:-1, 1:-1]
                             + face_coef[2] * grown[:, 1:-1, :-2, 1:-1] + face_coef[3] * grown[:, 1:-1, 2:, 1:-1]
                             + face_coef[4] * grown[:, 1:-1, 1:-1, :-2] + face_coef[5] * grown[:, 1:-1, 1:-1, 2:])
            velocity = (rhs + neighbour_sum) / diagonal
        flat_vel = jnp.pad(velocity, ((0, 0), (0, 1), (0, 1), (0, 0))).reshape(3, -1)
        marker_vel = jnp.zeros((3, SPHERES * MARK), jnp.float32)
        for index, weight in corner_list:
            marker_vel = marker_vel + weight[None] * flat_vel[:, index]
        marker_vel = marker_vel.reshape(3, SPHERES, MARK)
        push = jax.ops.segment_sum((pair_normal * contact_force[None]).T, own_index, SPHERES).T
        sphere_vel = jnp.mean(marker_vel, axis=2) + contact_gain * push
        multiplier = multiplier + rigid_step * (sphere_vel[:, :, None] - marker_vel)
        own_vel = sphere_vel[:, own_index]
        partner_vel = jnp.where(valid[None], sphere_vel[:, partner_index], jnp.float32(0.0))
        closing = jnp.sum(pair_normal * (partner_vel - own_vel), axis=0)
        contact_force = jnp.maximum(jnp.float32(0.0), contact_force - contact_step * (pair_gap + closing))
    return velocity, multiplier, contact_force
```

```python
import jax
import jax.numpy as jnp
from jax import lax
from jax.experimental import pallas as pl
from jax.experimental.pallas import tpu as pltpu
from jax.sharding import PartitionSpec as P

ITERS = 2
MESH = pl.DeviceIdType.MESH
F32 = jnp.float32
BF16 = jnp.bfloat16

CX, CY, NZ = 8, 8, 128
SPH, MARK = 2, 2048
CHUNK = 512
PER_SPHERE = MARK // CHUNK
CHUNKS = SPH * PER_SPHERE
ROWS = 88
PAD = 272
EXT = 13 * 16
HALO0, FORCE0, HALO1, FORCE1, RIGID0, RIGID1 = range(6)
OTHERS = [0, 1, 2, 3, 5, 6, 7, 8]


def row(x, y):
    return (x + 2) * 16 + y % 16


def split(value):
    high = value.astype(BF16)
    low = (value - high.astype(F32)).astype(BF16)
    return high, low


def body(
    vel, force, visc_class, table, mult, cell, frac, pair_sphere, pair_partner, normal, gap, contact,
    vel_out, mult_out, contact_out,
    own, ext, pack, halo_in, coef, rhs, grid, grid_pack, grid_diag, grid_in, diag_in,
    acc, share_acc, share, plane_w, depth_w, stack, left, mult_mid, rigid, rigid_in, normal8, contact_mid,
    send_sem, recv_sem,
):
    wide, narrow = lax.axis_index("wide"), lax.axis_index("narrow")
    n_wide, n_narrow = lax.axis_size("wide"), lax.axis_size("narrow")

    def neighbour(d):
        dx, dy = d // 3 - 1, d % 3 - 1
        return (lax.rem(wide + dx + n_wide, n_wide), lax.rem(narrow + dy + n_narrow, n_narrow))

    barrier = pltpu.get_barrier_semaphore()
    for d in OTHERS:
        pl.semaphore_signal(barrier, inc=1, device_id=neighbour(d), device_id_type=MESH)

    def transfer(kind, s, src, dst):
        return pltpu.make_async_remote_copy(
            src_ref=src, dst_ref=dst, send_sem=send_sem.at[kind, s], recv_sem=recv_sem.at[kind, s],
            device_id=neighbour(8 - s), device_id_type=MESH,
        )

    def halo_copies(turn):
        fields = 4 if turn == 0 else 3
        copies = []
        for s in OTHERS:
            dx, dy = s // 3 - 1, s % 3 - 1
            if dy == 0:
                rows = 24 if dx == 1 else 16
                start = 0 if dx == 1 else 48
                src = own.at[turn, 0:fields, start:start + rows]
            else:
                rows = 24 if dy == 1 else 16
                src = pack.at[turn, 0 if dy == 1 else 1, 0:fields, 0:rows]
            copies.append(transfer(HALO0 if turn == 0 else HALO1, s, src, halo_in.at[turn, s, 0:fields, 0:rows]))
        return copies

    def force_copies(turn):
        copies = []
        for s in OTHERS:
            dx, dy = s // 3 - 1, s % 3 - 1
            if dx != 0 and dy != 0:
                src, dst = grid_diag.at[turn, s], diag_in.at[turn, s]
            elif dy == 0:
                start = 0 if dx == 1 else 64
                src, dst = grid.at[turn, :, start:start + 24], grid_in.at[turn, s]
            else:
                src, dst = grid_pack.at[turn, 0 if dy == 1 else 1], grid_in.at[turn, s]
            copies.append(transfer(FORCE0 if turn == 0 else FORCE1, s, src, dst))
        return copies

    def rigid_copies(turn):
        return [
            transfer(RIGID0 if turn == 0 else RIGID1, s, rigid.at[turn], rigid_in.at[turn, s]) for s in OTHERS
        ]

    def start(copies):
        for copy in copies:
            copy.start()

    def arrive(copies):
        for copy in copies:
            copy.wait_recv()

    def leave(copies):
        for copy in copies:
            copy.wait_send()

    def pack_halo(turn):
        fields = 4 if turn == 0 else 3
        for f in range(fields):
            for j in range(3):
                pack[turn, 0, f, 8 * j:8 * j + 8, :] = own[turn, f, pl.ds(j, 8, stride=8), :]
            for j in range(2):
                pack[turn, 1, f, 8 * j:8 * j + 8, :] = own[turn, f, pl.ds(6 + j, 8, stride=8), :]

    def unpack_halo(turn):
        fields = 4 if turn == 0 else 3
        for f in range(fields):
            for i in range(3):
                ext[turn, f, pl.ds(row(8 + i, 0), 8), :] = halo_in[turn, 7, f, 8 * i:8 * i + 8, :]
            for i in range(2):
                ext[turn, f, pl.ds(row(i - 2, 0), 8), :] = halo_in[turn, 1, f, 8 * i:8 * i + 8, :]
            for j in range(3):
                ext[turn, f, pl.ds(row(0, 8 + j), 8, stride=16), :] = halo_in[turn, 5, f, 8 * j:8 * j + 8, :]
                ext[turn, f, pl.ds(row(8, 8 + j), 3, stride=16), :] = halo_in[turn, 8, f, 8 * j:8 * j + 3, :]
                ext[turn, f, pl.ds(row(-2, 8 + j), 2, stride=16), :] = halo_in[turn, 2, f, 8 * j + 6:8 * j + 8, :]
            for j in range(2):
                ext[turn, f, pl.ds(row(0, j - 2), 8, stride=16), :] = halo_in[turn, 3, f, 8 * j:8 * j + 8, :]
                ext[turn, f, pl.ds(row(8, j - 2), 3, stride=16), :] = halo_in[turn, 6, f, 8 * j:8 * j + 3, :]
                ext[turn, f, pl.ds(row(-2, j - 2), 2, stride=16), :] = halo_in[turn, 0, f, 8 * j + 6:8 * j + 8, :]

    classes = visc_class[...]
    mu = jnp.where(classes == 0, table[0], jnp.where(classes == 1, table[1], jnp.where(classes == 2, table[2], table[3])))
    mu = jnp.where((classes >= 0) & (classes <= 3), mu, F32(0.0))
    own[0, 3, :, :] = mu
    for c in range(3):
        own[0, c, :, :] = vel[c]
    for f in range(4):
        for x in range(8):
            ext[0, f, pl.ds(row(x, 0), 8), :] = own[0, f, 8 * x:8 * x + 8, :]
    pack_halo(0)

    pl.semaphore_wait(barrier, 8)
    start(halo_copies(0))

    acc[...] = jnp.zeros_like(acc)
    share_acc[...] = jnp.zeros_like(share_acc)

    def add_spread(lhs, depth):
        high, low = split(lhs)
        dims = (((1,), (1,)), ((), ()))
        return lax.dot_general(high, depth, dims, preferred_element_type=F32) + lax.dot_general(
            low, depth, dims, preferred_element_type=F32
        )

    def setup(n, carry):
        s, k = n // PER_SPHERE, n % PER_SPHERE
        lanes = pl.ds(pl.multiple_of(k * CHUNK, CHUNK), CHUNK)
        spot = cell[pl.ds(s, 1), lanes]
        cell_x, cell_y, cell_z = spot >> 10, (spot >> 7) & 7, spot & 127
        frac_x, frac_y, frac_z = (frac[a, pl.ds(s, 1), lanes] for a in range(3))
        gap_z = lax.broadcasted_iota(jnp.int32, (NZ, CHUNK), 0) - cell_z
        depth = jnp.where(gap_z == 0, 1.0 - frac_z, jnp.where(gap_z == 1, frac_z, F32(0.0)))
        depth_high, depth_low = split(depth)
        depth_w[n, 0:NZ, :] = depth_high
        depth_w[n, NZ:2 * NZ, :] = depth_low
        next_x = jnp.where(wide == n_wide - 1, F32(0.0), frac_x)
        next_y = jnp.where(narrow == n_narrow - 1, F32(0.0), frac_y)
        gap_8 = lax.broadcasted_iota(jnp.int32, (8, CHUNK), 0)
        weight_y = jnp.where(gap_8 == cell_y, 1.0 - frac_y, jnp.where(gap_8 == cell_y + 1, frac_y, F32(0.0)))
        weight_x = jnp.where(gap_8 == cell_x, 1.0 - frac_x, jnp.where(gap_8 == cell_x + 1, frac_x, F32(0.0)))
        last_x = jnp.where(cell_x == 7, next_x, F32(0.0))
        last_y = jnp.where(cell_y == 7, next_y, F32(0.0))
        tiles = [weight_x * last_y]
        for x in range(8):
            tiles.append(weight_x[x:x + 1] * weight_y)
        tiles.append(last_x * weight_y)
        corner = jnp.where(gap_8 == 0, weight_x[7:8], jnp.where(gap_8 == 1, last_x, F32(0.0))) * last_y
        tiles.append(corner)
        weight = jnp.concatenate(tiles, axis=0)
        plane_w[n] = weight
        lhs = [weight * (0.25 * mult[c, pl.ds(s, 1), lanes]) for c in range(3)]
        result = add_spread(jnp.concatenate(lhs + [weight], axis=0), depth_w[n])
        acc[0:264, :] += result[0:264]
        share_acc[s] += result[264:352]
        return carry

    lax.fori_loop(0, CHUNKS, setup, 0)
    for s in range(SPH):
        share[s] = (share_acc[s, :, 0:NZ] + share_acc[s, :, NZ:2 * NZ]) * F32(1.0 / MARK)

    def send_force(turn):
        for c in range(3):
            base = c * ROWS
            for t in range(11):
                part = acc[base + 8 * t:base + 8 * t + 8, 0:NZ] + acc[base + 8 * t:base + 8 * t + 8, NZ:2 * NZ]
                if 1 <= t <= 8:
                    part = part + force[c, 8 * t - 8:8 * t, :]
                grid[turn, c, 8 * t:8 * t + 8, :] = part
            for j in range(2):
                grid_pack[turn, 0, c, 8 * j:8 * j + 8, :] = grid[turn, c, pl.ds(8 + j, 8, stride=8), :]
            grid_pack[turn, 0, c, 16:24, :] = grid[turn, c, 72:80, :]
            grid_pack[turn, 1, c, 0:8, :] = grid[turn, c, pl.ds(15, 8, stride=8), :]
            grid_pack[turn, 1, c, 8:16, :] = grid[turn, c, 0:8, :]
            grid_pack[turn, 1, c, 16:17, :] = grid[turn, c, 79:80, :]
            grid_pack[turn, 1, c, 17:18, :] = grid[turn, c, 81:82, :]
            for s in (0, 2, 6, 8):
                dx, dy = s // 3 - 1, s % 3 - 1
                first = 8 if dx == 1 else 64
                for j in range(2):
                    if dy == 1:
                        rows = grid[turn, c, pl.ds(first + j, 2, stride=8), :]
                    elif j == 0:
                        rows = grid[turn, c, pl.ds(first + 7, 2, stride=8), :]
                    else:
                        at = 0 if dx == 1 else 80
                        rows = grid[turn, c, at:at + 2, :]
                    grid_diag[turn, s, 4 * c + 2 * j:4 * c + 2 * j + 2, :] = rows
        start(force_copies(turn))

    send_force(0)

    halos = halo_copies(0)
    arrive(halos)
    unpack_halo(0)
    row_id = lax.broadcasted_iota(jnp.int32, (16, NZ), 0)
    lane_id = lax.broadcasted_iota(jnp.int32, (16, NZ), 1)
    y_id = narrow * CY + jnp.where(row_id > 11, row_id - 16, row_id)

    def in_y(y):
        return (y >= 0) & (y < n_narrow * CY)

    def coefficients(i, carry):
        def viscosity(shift):
            x = wide * CX + i - 1 + shift
            inside = in_y(y_id) & (x >= 0) & (x < n_wide * CX)
            at = pl.multiple_of((i + 1 + shift) * 16, 16)
            return jnp.where(inside, ext[0, 3, pl.ds(at, 16), :], F32(0.0))

        mid = viscosity(0)
        x = wide * CX + i - 1
        around = [
            viscosity(-1),
            viscosity(1),
            jnp.where(in_y(y_id - 1), pltpu.roll(mid, 1, 0), F32(0.0)),
            jnp.where(in_y(y_id + 1), pltpu.roll(mid, 15, 0), F32(0.0)),
            jnp.where(lane_id == 0, F32(0.0), pltpu.roll(mid, 1, 1)),
            jnp.where(lane_id == NZ - 1, F32(0.0), pltpu.roll(mid, NZ - 1, 1)),
        ]
        valid = [
            (x - 1 >= 0) & (lane_id >= 0),
            (x + 1 < n_wide * CX) & (lane_id >= 0),
            in_y(y_id - 1),
            in_y(y_id + 1),
            lane_id > 0,
            lane_id < NZ - 1,
        ]
        faces = [0.5 * (mid + other) for other in around]
        diagonal = 1.0 + faces[0] + faces[1] + faces[2] + faces[3] + faces[4] + faces[5]
        inside = in_y(y_id) & (x >= 0) & (x < n_wide * CX)
        inverse = jnp.where(inside, 1.0 / diagonal, F32(0.0))
        at = pl.ds(pl.multiple_of(i * 16, 16), 16)
        for a in range(6):
            coef[a, at, :] = jnp.where(valid[a], faces[a] * inverse, F32(0.0))
        coef[6, at, :] = inverse
        return carry

    lax.fori_loop(0, 11, coefficients, 0)
    rhs[...] = jnp.zeros_like(rhs)
    stack[...] = jnp.zeros_like(stack)
    normal8[...] = jnp.zeros_like(normal8)
    normal8[0:3, :] = normal[...]
    normal8[4:7, :] = normal[...]

    sphere_row = lax.broadcasted_iota(jnp.int32, (8, 32), 0) // 4
    pair_s = pair_sphere[...].reshape(1, 32)
    pair_q = pair_partner[...].reshape(1, 32)
    contact_mid[...] = contact[...].reshape(1, 32)
    pair_gap = gap[...].reshape(1, 32)

    def gather_force(turn):
        arrive(force_copies(turn))
        for c in range(3):
            def add(x, y, n, stride, value):
                at = pl.ds(row(x, y), n, stride=stride) if stride != 1 else pl.ds(row(x, y), n)
                rhs[turn, c, at, :] += value

            for x in range(9):
                rhs[turn, c, pl.ds(row(x, 0), 8), :] = grid[turn, c, 8 + 8 * x:16 + 8 * x, :]
            rhs[turn, c, pl.ds(row(0, 8), 8, stride=16), :] = grid[turn, c, 0:8, :]
            rhs[turn, c, pl.ds(row(8, 8), 1), :] = grid[turn, c, 81:82, :]
            add(8, 0, 8, 1, grid_in[turn, 7, c, 8:16, :])
            add(9, 0, 8, 1, grid_in[turn, 7, c, 16:24, :])
            add(8, 8, 2, 16, grid_in[turn, 7, c, 0:2, :])
            add(-1, 0, 8, 1, grid_in[turn, 1, c, 0:8, :])
            add(0, 0, 8, 1, grid_in[turn, 1, c, 8:16, :])
            add(-1, 8, 2, 16, grid_in[turn, 1, c, 16:18, :])
            for s, low in ((5, 8), (3, -1)):
                for j in range(2):
                    add(0, low + j, 8, 16, grid_in[turn, s, c, 8 * j:8 * j + 8, :])
                    add(8, low + j, 1, 1, grid_in[turn, s, c, 16 + j:17 + j, :])
            for s in (0, 2, 6, 8):
                x = 8 if s // 3 == 2 else -1
                y = 8 if s % 3 == 2 else -1
                for j in range(2):
                    add(x, y + j, 2, 16, diag_in[turn, s, 4 * c + 2 * j:4 * c + 2 * j + 2, :])

    def sweep(source, target, first, count, turn):
        def one(i, carry):
            at = pl.ds(pl.multiple_of(i * 16, 16), 16)
            factors = [coef[a, at, :] for a in range(7)]
            for c in range(3):
                def load(shift):
                    return source[c, pl.ds(pl.multiple_of((i + 1 + shift) * 16, 16), 16), :]

                mid = load(0)
                value = factors[6] * rhs[turn, c, pl.ds(pl.multiple_of((i + 1) * 16, 16), 16), :]
                value += factors[0] * load(-1)
                value += factors[1] * load(1)
                value += factors[2] * pltpu.roll(mid, 1, 0)
                value += factors[3] * pltpu.roll(mid, 15, 0)
                value += factors[4] * pltpu.roll(mid, 1, 1)
                value += factors[5] * pltpu.roll(mid, NZ - 1, 1)
                target[c, pl.ds(pl.multiple_of((i + 1) * 16, 16), 16), :] = value
            return carry

        lax.fori_loop(first, first + count, one, 0)

    def update_contact(turn):
        quarter = pair_q // 2
        partner = jnp.zeros((8, 32), F32)
        for q in range(9):
            if q == 4:
                tile = rigid[turn, :, 0:32]
            else:
                qx, qy = q // 3 - 1, q % 3 - 1
                inside = (wide + qx >= 0) & (wide + qx < n_wide) & (narrow + qy >= 0) & (narrow + qy < n_narrow)
                tile = jnp.where(inside, rigid_in[turn, q, :, 0:32], F32(0.0))
            partner = jnp.where(quarter == q, tile, partner)
        closing8 = jnp.where(sphere_row == pair_q - 2 * quarter, partner, F32(0.0)) - jnp.where(
            sphere_row == pair_s, rigid[turn, :, 0:32], F32(0.0)
        )
        closing = jnp.sum(normal8[...] * closing8, axis=0, keepdims=True)
        return jnp.maximum(F32(0.0), contact_mid[...] - 0.5 * (pair_gap + closing))

    for turn in range(ITERS):
        last = turn == ITERS - 1
        if turn > 0:
            arrive(halo_copies(turn))
            unpack_halo(turn)
        gather_force(turn)
        middle = ext.at[2]
        sweep(ext.at[turn], middle, 0, 11, turn)
        sweep(middle, ext.at[3], 1, 9, turn)
        done = ext.at[3]
        for c in range(3):
            for x in range(9):
                tile = done[c, pl.ds(row(x, 0), 8), :]
                stack[c * ROWS + 8 + 8 * x:c * ROWS + 16 + 8 * x, :] = tile
                if x < 8:
                    if last:
                        vel_out[c, 8 * x:8 * x + 8, :] = tile
                    else:
                        own[turn + 1, c, 8 * x:8 * x + 8, :] = tile
                        ext[turn + 1, c, pl.ds(row(x, 0), 8), :] = tile
            stack[c * ROWS:c * ROWS + 8, :] = done[c, pl.ds(row(0, 8), 8, stride=16), :]
            stack[c * ROWS + 81:c * ROWS + 82, :] = done[c, pl.ds(row(8, 8), 1), :]
        if not last:
            pack_halo(turn + 1)
            start(halo_copies(turn + 1))
        if turn > 0:
            arrive(rigid_copies(turn - 1))
            contact_mid[...] = update_contact(turn - 1)
        sums = jnp.zeros((8, NZ), F32)
        row8 = lax.broadcasted_iota(jnp.int32, (8, NZ), 0)
        for s in range(SPH):
            for c in range(3):
                part = jnp.sum(share[s] * stack[c * ROWS:(c + 1) * ROWS, :], axis=0, keepdims=True)
                sums = jnp.where(row8 == 4 * s + c, part, sums)
        push = jnp.where(sphere_row == pair_s, normal8[...] * contact_mid[...], F32(0.0))
        speed = jnp.sum(sums, axis=1, keepdims=True) + 0.5 * jnp.sum(push, axis=1, keepdims=True)
        rigid[turn] = jnp.broadcast_to(speed, (8, NZ))
        start(rigid_copies(turn))
        high, low = split(stack[...])
        left[0:PAD, 0:NZ] = high
        left[0:PAD, NZ:2 * NZ] = high
        left[PAD:2 * PAD, 0:NZ] = low
        left[PAD:2 * PAD, NZ:2 * NZ] = low
        if not last:
            acc[...] = jnp.zeros_like(acc)
        source = mult if turn == 0 else mult_mid

        def markers(n, carry):
            s, k = n // PER_SPHERE, n % PER_SPHERE
            lanes = pl.ds(pl.multiple_of(k * CHUNK, CHUNK), CHUNK)
            weight = plane_w[n]
            sampled = jnp.dot(left[...], depth_w[n], preferred_element_type=F32)
            lhs = []
            for c in range(3):
                rows = slice(c * ROWS, (c + 1) * ROWS)
                low_rows = slice(PAD + c * ROWS, PAD + (c + 1) * ROWS)
                read = jnp.sum((sampled[rows] + sampled[low_rows]) * weight, axis=0, keepdims=True)
                speed = rigid[turn, pl.ds(4 * s + c, 1), 0:1]
                new = source[c, pl.ds(s, 1), lanes] + 0.5 * (speed - read)
                if last:
                    mult_out[c, pl.ds(s, 1), lanes] = new
                else:
                    mult_mid[c, pl.ds(s, 1), lanes] = new
                    lhs.append(weight * (0.25 * new))
            if not last:
                lhs.append(jnp.zeros((8, CHUNK), F32))
                acc[...] += add_spread(jnp.concatenate(lhs, axis=0), depth_w[n])
            return carry

        lax.fori_loop(0, CHUNKS, markers, 0)
        if not last:
            send_force(turn + 1)
    arrive(rigid_copies(ITERS - 1))
    contact_out[...] = update_contact(ITERS - 1).reshape(32)
    for turn in range(ITERS):
        leave(halo_copies(turn))
        leave(force_copies(turn))
        leave(rigid_copies(turn))


def local(
    velocity, force, visc_class, visc_table, multiplier, marker_cell, marker_frac,
    pair_sphere, pair_partner, pair_normal, pair_gap, contact_force,
):
    comps = 3
    vmem = pl.BlockSpec(memory_space=pltpu.VMEM)
    specs = [vmem] * 12
    specs[3] = pl.BlockSpec(memory_space=pltpu.SMEM)
    out = pl.pallas_call(
        body,
        out_shape=(
            jax.ShapeDtypeStruct((comps, CX * CY, NZ), F32),
            jax.ShapeDtypeStruct(multiplier.shape, F32),
            jax.ShapeDtypeStruct(contact_force.shape, F32),
        ),
        in_specs=specs,
        out_specs=(vmem, vmem, vmem),
        scratch_shapes=[
            pltpu.VMEM((2, 4, CX * CY, NZ), F32),
            pltpu.VMEM((4, 4, EXT, NZ), F32),
            pltpu.VMEM((2, 2, 4, 24, NZ), F32),
            pltpu.VMEM((2, 9, 4, 24, NZ), F32),
            pltpu.VMEM((7, 11 * 16, NZ), F32),
            pltpu.VMEM((2, comps, EXT, NZ), F32),
            pltpu.VMEM((2, comps, ROWS, NZ), F32),
            pltpu.VMEM((2, 2, comps, 24, NZ), F32),
            pltpu.VMEM((2, 9, 16, NZ), F32),
            pltpu.VMEM((2, 9, comps, 24, NZ), F32),
            pltpu.VMEM((2, 9, 16, NZ), F32),
            pltpu.VMEM((PAD, 2 * NZ), F32),
            pltpu.VMEM((SPH, ROWS, 2 * NZ), F32),
            pltpu.VMEM((SPH, ROWS, NZ), F32),
            pltpu.VMEM((CHUNKS, ROWS, CHUNK), F32),
            pltpu.VMEM((CHUNKS, 2 * NZ, CHUNK), BF16),
            pltpu.VMEM((PAD, NZ), F32),
            pltpu.VMEM((2 * PAD, 2 * NZ), BF16),
            pltpu.VMEM((comps, SPH, MARK), F32),
            pltpu.VMEM((2, 8, NZ), F32),
            pltpu.VMEM((2, 9, 8, NZ), F32),
            pltpu.VMEM((8, 32), F32),
            pltpu.VMEM((1, 32), F32),
            pltpu.SemaphoreType.DMA((6, 9)),
            pltpu.SemaphoreType.DMA((6, 9)),
        ],
        compiler_params=pltpu.CompilerParams(
            collective_id=0, has_side_effects=True, vmem_limit_bytes=48 * 1024 * 1024
        ),
    )(
        velocity.reshape(comps, CX * CY, NZ), force.reshape(comps, CX * CY, NZ), visc_class.reshape(CX * CY, NZ),
        visc_table, multiplier, marker_cell, marker_frac, pair_sphere, pair_partner, pair_normal, pair_gap, contact_force,
    )
    return (out[0].reshape(comps, CX, CY, NZ), out[1], out[2])


def solution(mesh):
    in_specs = (
        P(None, "wide", "narrow", None),
        P(None, "wide", "narrow", None),
        P("wide", "narrow", None),
        P(),
        P(None, ("wide", "narrow"), None),
        P(("wide", "narrow"), None),
        P(None, ("wide", "narrow"), None),
        P(("wide", "narrow")),
        P(("wide", "narrow")),
        P(None, ("wide", "narrow")),
        P(("wide", "narrow")),
        P(("wide", "narrow")),
    )
    out_specs = (
        P(None, "wide", "narrow", None),
        P(None, ("wide", "narrow"), None),
        P(("wide", "narrow")),
    )
    return jax.shard_map(local, mesh=mesh, in_specs=in_specs, out_specs=out_specs, check_vma=False)
```

```python
import jax
import jax.numpy as jnp
from jax import lax
from jax.experimental import pallas as pl
from jax.experimental.pallas import tpu as pltpu
from jax.sharding import PartitionSpec as P

ITERS = 2
MESH = pl.DeviceIdType.MESH
F32 = jnp.float32
BF16 = jnp.bfloat16

CX, CY, NZ = 8, 8, 128
SPH, MARK = 2, 2048
CHUNK = 256
PER_SPHERE = MARK // CHUNK
CHUNKS = SPH * PER_SPHERE
ROWS = 88
PAD = 272
EXT = 13 * 16
HALO0, FORCE0, HALO1, FORCE1, RIGID0, RIGID1 = range(6)
OTHERS = [0, 1, 2, 3, 5, 6, 7, 8]


def row(x, y):
    return (x + 2) * 16 + y % 16


def span(direction):
    return (0, 1, 2) if direction == 1 else (6, 7)


def split(value):
    high = value.astype(BF16)
    low = (value - high.astype(F32)).astype(BF16)
    return high, low


def body(
    vel_hbm, force_hbm, class_hbm, table_hbm, mult_hbm, cell_hbm, frac_hbm, sphere_hbm, partner_hbm, normal_hbm, gap_hbm,
    contact_hbm, vel_hbm_out, mult_hbm_out, contact_hbm_out,
    own, ext, pack, halo_in, halo_diag, halo_diag_in, coef, rhs, grid, grid_pack, grid_diag, grid_in, diag_in,
    visc_class, table, cell, frac, mult, force, pair_sphere, pair_partner, normal, gap, contact,
    acc, share_acc, share, plane_w, depth_w, stack, left, mult_mid, rigid, rigid_in, normal8, contact_mid,
    vel_out, mult_out, contact_out, load_sem, send_sem, recv_sem,
):
    wide, narrow = lax.axis_index("wide"), lax.axis_index("narrow")
    n_wide, n_narrow = lax.axis_size("wide"), lax.axis_size("narrow")

    def neighbour(d):
        dx, dy = d // 3 - 1, d % 3 - 1
        return (lax.rem(wide + dx + n_wide, n_wide), lax.rem(narrow + dy + n_narrow, n_narrow))

    def exists(d):
        dx, dy = d // 3 - 1, d % 3 - 1
        return (wide + dx >= 0) & (wide + dx < n_wide) & (narrow + dy >= 0) & (narrow + dy < n_narrow)

    barrier = pltpu.get_barrier_semaphore()
    for d in OTHERS:
        @pl.when(exists(d))
        def greet(d=d):
            pl.semaphore_signal(barrier, inc=1, device_id=neighbour(d), device_id_type=MESH)
    across = jnp.where(wide > 0, 1, 0) + jnp.where(wide < n_wide - 1, 1, 0) + 1
    along = jnp.where(narrow > 0, 1, 0) + jnp.where(narrow < n_narrow - 1, 1, 0) + 1

    loads = [
        pltpu.make_async_copy(src, dst, load_sem.at[k])
        for k, (src, dst) in enumerate((
            (class_hbm, visc_class), (table_hbm, table), (vel_hbm, own.at[0, 0:3]), (cell_hbm, cell), (frac_hbm, frac),
            (mult_hbm, mult), (force_hbm, force), (sphere_hbm, pair_sphere), (partner_hbm, pair_partner),
            (normal_hbm, normal), (gap_hbm, gap), (contact_hbm, contact),
        ))
    ]
    for load in loads:
        load.start()
    stores = [
        pltpu.make_async_copy(src, dst, load_sem.at[12 + k])
        for k, (src, dst) in enumerate(((vel_out, vel_hbm_out), (mult_out, mult_hbm_out), (contact_out, contact_hbm_out)))
    ]

    def transfer(kind, s, src, dst):
        return pltpu.make_async_remote_copy(
            src_ref=src, dst_ref=dst, send_sem=send_sem.at[kind, s], recv_sem=recv_sem.at[kind, s],
            device_id=neighbour(8 - s), device_id_type=MESH,
        )

    def halo_copies(turn):
        fields = 4 if turn == 0 else 3
        copies = []
        for s in OTHERS:
            dx, dy = s // 3 - 1, s % 3 - 1
            if dx != 0 and dy != 0:
                count = fields * len(span(dx)) * len(span(dy))
                rows = (count + 7) // 8 * 8
                copies.append(transfer(HALO0 if turn == 0 else HALO1, s, halo_diag.at[turn, s, 0:rows], halo_diag_in.at[turn, s, 0:rows]))
                continue
            if dy == 0:
                rows = 24 if dx == 1 else 16
                first = 0 if dx == 1 else 48
                src = own.at[turn, 0:fields, first:first + rows]
            else:
                rows = 24 if dy == 1 else 16
                src = pack.at[turn, 0 if dy == 1 else 1, 0:fields, 0:rows]
            copies.append(transfer(HALO0 if turn == 0 else HALO1, s, src, halo_in.at[turn, s, 0:fields, 0:rows]))
        return copies

    def force_copies(turn):
        copies = []
        for s in OTHERS:
            dx, dy = s // 3 - 1, s % 3 - 1
            if dx != 0 and dy != 0:
                src, dst = grid_diag.at[turn, s], diag_in.at[turn, s]
            elif dy == 0:
                start = 0 if dx == 1 else 64
                src, dst = grid.at[turn, :, start:start + 24], grid_in.at[turn, s]
            else:
                src, dst = grid_pack.at[turn, 0 if dy == 1 else 1], grid_in.at[turn, s]
            copies.append(transfer(FORCE0 if turn == 0 else FORCE1, s, src, dst))
        return copies

    def rigid_copies(turn):
        return [
            transfer(RIGID0 if turn == 0 else RIGID1, s, rigid.at[turn], rigid_in.at[turn, s]) for s in OTHERS
        ]

    def start(copies):
        for s, copy in zip(OTHERS, copies):
            @pl.when(exists(8 - s))
            def go(copy=copy):
                copy.start()

    def arrive(copies):
        for s, copy in zip(OTHERS, copies):
            @pl.when(exists(s))
            def go(copy=copy):
                copy.wait_recv()

    def leave(copies):
        for s, copy in zip(OTHERS, copies):
            @pl.when(exists(8 - s))
            def go(copy=copy):
                copy.wait_send()

    def received(s, value):
        return jnp.where(exists(s), value, F32(0.0))

    def pack_halo(turn):
        fields = 4 if turn == 0 else 3
        for f in range(fields):
            for j in range(3):
                pack[turn, 0, f, 8 * j:8 * j + 8, :] = own[turn, f, pl.ds(j, 8, stride=8), :]
            for j in range(2):
                pack[turn, 1, f, 8 * j:8 * j + 8, :] = own[turn, f, pl.ds(6 + j, 8, stride=8), :]

        for s in (0, 2, 6, 8):
            xs, ys = span(s // 3 - 1), span(s % 3 - 1)
            for f in range(fields):
                for j, y in enumerate(ys):
                    at = (f * len(ys) + j) * len(xs)
                    halo_diag[turn, s, at:at + len(xs), :] = own[turn, f, pl.ds(xs[0] * 8 + y, len(xs), stride=8), :]

    def unpack_halo(turn):
        fields = 4 if turn == 0 else 3
        for f in range(fields):
            for i in range(3):
                ext[turn, f, pl.ds(row(8 + i, 0), 8), :] = received(7, halo_in[turn, 7, f, 8 * i:8 * i + 8, :])
            for i in range(2):
                ext[turn, f, pl.ds(row(i - 2, 0), 8), :] = received(1, halo_in[turn, 1, f, 8 * i:8 * i + 8, :])
            for j in range(3):
                ext[turn, f, pl.ds(row(0, 8 + j), 8, stride=16), :] = received(5, halo_in[turn, 5, f, 8 * j:8 * j + 8, :])
            for j in range(2):
                ext[turn, f, pl.ds(row(0, j - 2), 8, stride=16), :] = received(3, halo_in[turn, 3, f, 8 * j:8 * j + 8, :])
            for s in (0, 2, 6, 8):
                xs, ys = span(s // 3 - 1), span(s % 3 - 1)
                x0 = 8 if s // 3 == 2 else -2
                y0 = 8 if s % 3 == 2 else -2
                for j in range(len(ys)):
                    at = (f * len(ys) + j) * len(xs)
                    ext[turn, f, pl.ds(row(x0, y0 + j), len(xs), stride=16), :] = received(
                        s, halo_diag_in[turn, s, at:at + len(xs), :]
                    )

    for load in loads[0:3]:
        load.wait()
    classes = visc_class[...]
    mu = jnp.where(classes == 0, table[0], jnp.where(classes == 1, table[1], jnp.where(classes == 2, table[2], table[3])))
    mu = jnp.where((classes >= 0) & (classes <= 3), mu, F32(0.0))
    own[0, 3, :, :] = mu
    for f in range(4):
        for x in range(8):
            ext[0, f, pl.ds(row(x, 0), 8), :] = own[0, f, 8 * x:8 * x + 8, :]
    pack_halo(0)

    pl.semaphore_wait(barrier, across * along - 1)
    start(halo_copies(0))

    for load in loads[3:]:
        load.wait()
    acc[...] = jnp.zeros_like(acc)
    share_acc[...] = jnp.zeros_like(share_acc)

    def add_spread(lhs, depth):
        high, low = split(lhs)
        dims = (((1,), (1,)), ((), ()))
        return lax.dot_general(high, depth, dims, preferred_element_type=F32) + lax.dot_general(
            low, depth, dims, preferred_element_type=F32
        )

    def setup(n, carry):
        s, k = n // PER_SPHERE, n % PER_SPHERE
        lanes = pl.ds(pl.multiple_of(k * CHUNK, CHUNK), CHUNK)
        spot = cell[pl.ds(s, 1), lanes]
        cell_x, cell_y, cell_z = spot >> 10, (spot >> 7) & 7, spot & 127
        frac_x, frac_y, frac_z = (frac[a, pl.ds(s, 1), lanes] for a in range(3))
        gap_z = lax.broadcasted_iota(jnp.int32, (NZ, CHUNK), 0) - cell_z
        depth = jnp.where(gap_z == 0, 1.0 - frac_z, jnp.where(gap_z == 1, frac_z, F32(0.0)))
        depth_high, depth_low = split(depth)
        depth_w[n, 0:NZ, :] = depth_high
        depth_w[n, NZ:2 * NZ, :] = depth_low
        next_x = jnp.where(wide == n_wide - 1, F32(0.0), frac_x)
        next_y = jnp.where(narrow == n_narrow - 1, F32(0.0), frac_y)
        gap_8 = lax.broadcasted_iota(jnp.int32, (8, CHUNK), 0)
        weight_y = jnp.where(gap_8 == cell_y, 1.0 - frac_y, jnp.where(gap_8 == cell_y + 1, frac_y, F32(0.0)))
        weight_x = jnp.where(gap_8 == cell_x, 1.0 - frac_x, jnp.where(gap_8 == cell_x + 1, frac_x, F32(0.0)))
        last_x = jnp.where(cell_x == 7, next_x, F32(0.0))
        last_y = jnp.where(cell_y == 7, next_y, F32(0.0))
        tiles = [weight_x * last_y]
        for x in range(8):
            tiles.append(weight_x[x:x + 1] * weight_y)
        tiles.append(last_x * weight_y)
        corner = jnp.where(gap_8 == 0, weight_x[7:8], jnp.where(gap_8 == 1, last_x, F32(0.0))) * last_y
        tiles.append(corner)
        weight = jnp.concatenate(tiles, axis=0)
        plane_w[n] = weight
        lhs = [weight * (0.25 * mult[c, pl.ds(s, 1), lanes]) for c in range(3)]
        result = add_spread(jnp.concatenate(lhs + [weight], axis=0), depth_w[n])
        acc[0:264, :] += result[0:264]
        share_acc[s] += result[264:352]
        return carry

    lax.fori_loop(0, CHUNKS, setup, 0, unroll=8)
    for s in range(SPH):
        share[s] = (share_acc[s, :, 0:NZ] + share_acc[s, :, NZ:2 * NZ]) * F32(1.0 / MARK)

    def send_force(turn):
        for c in range(3):
            base = c * ROWS
            for t in range(11):
                part = acc[base + 8 * t:base + 8 * t + 8, 0:NZ] + acc[base + 8 * t:base + 8 * t + 8, NZ:2 * NZ]
                if 1 <= t <= 8:
                    part = part + force[c, 8 * t - 8:8 * t, :]
                grid[turn, c, 8 * t:8 * t + 8, :] = part
            for j in range(2):
                grid_pack[turn, 0, c, 8 * j:8 * j + 8, :] = grid[turn, c, pl.ds(8 + j, 8, stride=8), :]
            grid_pack[turn, 0, c, 16:24, :] = grid[turn, c, 72:80, :]
            grid_pack[turn, 1, c, 0:8, :] = grid[turn, c, pl.ds(15, 8, stride=8), :]
            grid_pack[turn, 1, c, 8:16, :] = grid[turn, c, 0:8, :]
            grid_pack[turn, 1, c, 16:17, :] = grid[turn, c, 79:80, :]
            grid_pack[turn, 1, c, 17:18, :] = grid[turn, c, 81:82, :]
            for s in (0, 2, 6, 8):
                dx, dy = s // 3 - 1, s % 3 - 1
                first = 8 if dx == 1 else 64
                for j in range(2):
                    if dy == 1:
                        rows = grid[turn, c, pl.ds(first + j, 2, stride=8), :]
                    elif j == 0:
                        rows = grid[turn, c, pl.ds(first + 7, 2, stride=8), :]
                    else:
                        at = 0 if dx == 1 else 80
                        rows = grid[turn, c, at:at + 2, :]
                    grid_diag[turn, s, 4 * c + 2 * j:4 * c + 2 * j + 2, :] = rows
        start(force_copies(turn))

    send_force(0)

    halos = halo_copies(0)
    arrive(halos)
    unpack_halo(0)
    row_id = lax.broadcasted_iota(jnp.int32, (16, NZ), 0)
    lane_id = lax.broadcasted_iota(jnp.int32, (16, NZ), 1)
    y_id = narrow * CY + jnp.where(row_id > 11, row_id - 16, row_id)

    def in_y(y):
        return (y >= 0) & (y < n_narrow * CY)

    def coefficients(i, carry):
        def viscosity(shift):
            x = wide * CX + i - 1 + shift
            inside = in_y(y_id) & (x >= 0) & (x < n_wide * CX)
            at = pl.multiple_of((i + 1 + shift) * 16, 16)
            return jnp.where(inside, ext[0, 3, pl.ds(at, 16), :], F32(0.0))

        mid = viscosity(0)
        x = wide * CX + i - 1
        around = [
            viscosity(-1),
            viscosity(1),
            jnp.where(in_y(y_id - 1), pltpu.roll(mid, 1, 0), F32(0.0)),
            jnp.where(in_y(y_id + 1), pltpu.roll(mid, 15, 0), F32(0.0)),
            jnp.where(lane_id == 0, F32(0.0), pltpu.roll(mid, 1, 1)),
            jnp.where(lane_id == NZ - 1, F32(0.0), pltpu.roll(mid, NZ - 1, 1)),
        ]
        valid = [
            (x - 1 >= 0) & (lane_id >= 0),
            (x + 1 < n_wide * CX) & (lane_id >= 0),
            in_y(y_id - 1),
            in_y(y_id + 1),
            lane_id > 0,
            lane_id < NZ - 1,
        ]
        faces = [0.5 * (mid + other) for other in around]
        diagonal = 1.0 + faces[0] + faces[1] + faces[2] + faces[3] + faces[4] + faces[5]
        inside = in_y(y_id) & (x >= 0) & (x < n_wide * CX)
        inverse = jnp.where(inside, 1.0 / diagonal, F32(0.0))
        at = pl.ds(pl.multiple_of(i * 16, 16), 16)
        for a in range(6):
            coef[a, at, :] = jnp.where(valid[a], faces[a] * inverse, F32(0.0))
        coef[6, at, :] = inverse
        return carry

    lax.fori_loop(0, 11, coefficients, 0, unroll=True)
    rhs[...] = jnp.zeros_like(rhs)
    stack[...] = jnp.zeros_like(stack)
    normal8[...] = jnp.zeros_like(normal8)
    normal8[0:3, :] = normal[...]
    normal8[4:7, :] = normal[...]

    sphere_row = lax.broadcasted_iota(jnp.int32, (8, 32), 0) // 4
    pair_s = pair_sphere[...].reshape(1, 32)
    pair_q = pair_partner[...].reshape(1, 32)
    contact_mid[...] = contact[...].reshape(1, 32)
    pair_gap = gap[...].reshape(1, 32)

    def gather_force(turn):
        arrive(force_copies(turn))
        for c in range(3):
            def add(x, y, n, stride, value):
                at = pl.ds(row(x, y), n, stride=stride) if stride != 1 else pl.ds(row(x, y), n)
                rhs[turn, c, at, :] += value

            for x in range(9):
                rhs[turn, c, pl.ds(row(x, 0), 8), :] = grid[turn, c, 8 + 8 * x:16 + 8 * x, :]
            rhs[turn, c, pl.ds(row(0, 8), 8, stride=16), :] = grid[turn, c, 0:8, :]
            rhs[turn, c, pl.ds(row(8, 8), 1), :] = grid[turn, c, 81:82, :]
            add(8, 0, 8, 1, received(7, grid_in[turn, 7, c, 8:16, :]))
            add(9, 0, 8, 1, received(7, grid_in[turn, 7, c, 16:24, :]))
            add(8, 8, 2, 16, received(7, grid_in[turn, 7, c, 0:2, :]))
            add(-1, 0, 8, 1, received(1, grid_in[turn, 1, c, 0:8, :]))
            add(0, 0, 8, 1, received(1, grid_in[turn, 1, c, 8:16, :]))
            add(-1, 8, 2, 16, received(1, grid_in[turn, 1, c, 16:18, :]))
            for s, low in ((5, 8), (3, -1)):
                for j in range(2):
                    add(0, low + j, 8, 16, received(s, grid_in[turn, s, c, 8 * j:8 * j + 8, :]))
                    add(8, low + j, 1, 1, received(s, grid_in[turn, s, c, 16 + j:17 + j, :]))
            for s in (0, 2, 6, 8):
                x = 8 if s // 3 == 2 else -1
                y = 8 if s % 3 == 2 else -1
                for j in range(2):
                    add(x, y + j, 2, 16, received(s, diag_in[turn, s, 4 * c + 2 * j:4 * c + 2 * j + 2, :]))

    def sweep(source, target, first, count, turn):
        def one(i, carry):
            at = pl.ds(pl.multiple_of(i * 16, 16), 16)
            factors = [coef[a, at, :] for a in range(7)]
            for c in range(3):
                def load(shift):
                    return source[c, pl.ds(pl.multiple_of((i + 1 + shift) * 16, 16), 16), :]

                mid = load(0)
                value = factors[6] * rhs[turn, c, pl.ds(pl.multiple_of((i + 1) * 16, 16), 16), :]
                value += factors[0] * load(-1)
                value += factors[1] * load(1)
                value += factors[2] * pltpu.roll(mid, 1, 0)
                value += factors[3] * pltpu.roll(mid, 15, 0)
                value += factors[4] * pltpu.roll(mid, 1, 1)
                value += factors[5] * pltpu.roll(mid, NZ - 1, 1)
                target[c, pl.ds(pl.multiple_of((i + 1) * 16, 16), 16), :] = value
            return carry

        lax.fori_loop(first, first + count, one, 0, unroll=True)

    def update_contact(turn):
        quarter = pair_q // 2
        partner = jnp.zeros((8, 32), F32)
        for q in range(9):
            if q == 4:
                tile = rigid[turn, :, 0:32]
            else:
                tile = received(q, rigid_in[turn, q, :, 0:32])
            partner = jnp.where(quarter == q, tile, partner)
        closing8 = jnp.where(sphere_row == pair_q - 2 * quarter, partner, F32(0.0)) - jnp.where(
            sphere_row == pair_s, rigid[turn, :, 0:32], F32(0.0)
        )
        closing = jnp.sum(normal8[...] * closing8, axis=0, keepdims=True)
        return jnp.maximum(F32(0.0), contact_mid[...] - 0.5 * (pair_gap + closing))

    for turn in range(ITERS):
        last = turn == ITERS - 1
        if turn > 0:
            arrive(halo_copies(turn))
            unpack_halo(turn)
        gather_force(turn)
        middle = ext.at[2]
        sweep(ext.at[turn], middle, 0, 11, turn)
        sweep(middle, ext.at[3], 1, 9, turn)
        done = ext.at[3]
        for c in range(3):
            for x in range(9):
                tile = done[c, pl.ds(row(x, 0), 8), :]
                stack[c * ROWS + 8 + 8 * x:c * ROWS + 16 + 8 * x, :] = tile
                if x < 8:
                    if last:
                        vel_out[c, 8 * x:8 * x + 8, :] = tile
                    else:
                        own[turn + 1, c, 8 * x:8 * x + 8, :] = tile
                        ext[turn + 1, c, pl.ds(row(x, 0), 8), :] = tile
            stack[c * ROWS:c * ROWS + 8, :] = done[c, pl.ds(row(0, 8), 8, stride=16), :]
            stack[c * ROWS + 81:c * ROWS + 82, :] = done[c, pl.ds(row(8, 8), 1), :]
        if not last:
            pack_halo(turn + 1)
            start(halo_copies(turn + 1))
        if turn > 0:
            arrive(rigid_copies(turn - 1))
            contact_mid[...] = update_contact(turn - 1)
        if last:
            stores[0].start()
        sums = jnp.zeros((8, NZ), F32)
        row8 = lax.broadcasted_iota(jnp.int32, (8, NZ), 0)
        for s in range(SPH):
            for c in range(3):
                part = jnp.sum(share[s] * stack[c * ROWS:(c + 1) * ROWS, :], axis=0, keepdims=True)
                sums = jnp.where(row8 == 4 * s + c, part, sums)
        push = jnp.where(sphere_row == pair_s, normal8[...] * contact_mid[...], F32(0.0))
        speed = jnp.sum(sums, axis=1, keepdims=True) + 0.5 * jnp.sum(push, axis=1, keepdims=True)
        rigid[turn] = jnp.broadcast_to(speed, (8, NZ))
        start(rigid_copies(turn))
        high, low = split(stack[...])
        left[0:PAD, 0:NZ] = high
        left[0:PAD, NZ:2 * NZ] = high
        left[PAD:2 * PAD, 0:NZ] = low
        left[PAD:2 * PAD, NZ:2 * NZ] = low
        if not last:
            acc[...] = jnp.zeros_like(acc)
        source = mult if turn == 0 else mult_mid

        def markers(n, carry):
            s, k = n // PER_SPHERE, n % PER_SPHERE
            lanes = pl.ds(pl.multiple_of(k * CHUNK, CHUNK), CHUNK)
            weight = plane_w[n]
            sampled = jnp.dot(left[0:PAD], depth_w[n], preferred_element_type=F32) + jnp.dot(left[PAD:2 * PAD], depth_w[n], preferred_element_type=F32)
            lhs = []
            for c in range(3):
                rows = slice(c * ROWS, (c + 1) * ROWS)
                low_rows = slice(PAD + c * ROWS, PAD + (c + 1) * ROWS)
                read = jnp.sum(sampled[rows] * weight, axis=0, keepdims=True)
                speed = rigid[turn, pl.ds(4 * s + c, 1), 0:1]
                new = source[c, pl.ds(s, 1), lanes] + 0.5 * (speed - read)
                if last:
                    mult_out[c, pl.ds(s, 1), lanes] = new
                else:
                    mult_mid[c, pl.ds(s, 1), lanes] = new
                    lhs.append(weight * (0.25 * new))
            if not last:
                lhs.append(jnp.zeros((8, CHUNK), F32))
                acc[...] += add_spread(jnp.concatenate(lhs, axis=0), depth_w[n])
            return carry

        lax.fori_loop(0, CHUNKS, markers, 0, unroll=8)
        if not last:
            send_force(turn + 1)
    stores[1].start()
    arrive(rigid_copies(ITERS - 1))
    contact_out[...] = update_contact(ITERS - 1).reshape(32)
    stores[2].start()
    for turn in range(ITERS):
        leave(halo_copies(turn))
        leave(force_copies(turn))
        leave(rigid_copies(turn))
    for store in stores:
        store.wait()


def hand_over(vel, mult, contact, vel_out, mult_out, contact_out, sem):
    copies = [
        pltpu.make_async_copy(src, dst, sem.at[k])
        for k, (src, dst) in enumerate(((vel, vel_out), (mult, mult_out), (contact, contact_out)))
    ]
    for copy in copies:
        copy.start()
    for copy in copies:
        copy.wait()


def local(
    velocity, force, visc_class, visc_table, multiplier, marker_cell, marker_frac,
    pair_sphere, pair_partner, pair_normal, pair_gap, contact_force,
):
    comps = 3
    hbm = pl.BlockSpec(memory_space=pltpu.MemorySpace.HBM)
    out_shape = (
        jax.ShapeDtypeStruct((comps, CX * CY, NZ), F32),
        jax.ShapeDtypeStruct(multiplier.shape, F32),
        jax.ShapeDtypeStruct(contact_force.shape, F32),
    )
    out = pl.pallas_call(
        body,
        out_shape=out_shape,
        in_specs=[hbm] * 12,
        out_specs=(hbm, hbm, hbm),
        scratch_shapes=[
            pltpu.VMEM((2, 4, CX * CY, NZ), F32),
            pltpu.VMEM((4, 4, EXT, NZ), F32),
            pltpu.VMEM((2, 2, 4, 24, NZ), F32),
            pltpu.VMEM((2, 9, 4, 24, NZ), F32),
            pltpu.VMEM((2, 9, 40, NZ), F32),
            pltpu.VMEM((2, 9, 40, NZ), F32),
            pltpu.VMEM((7, 11 * 16, NZ), F32),
            pltpu.VMEM((2, comps, EXT, NZ), F32),
            pltpu.VMEM((2, comps, ROWS, NZ), F32),
            pltpu.VMEM((2, 2, comps, 24, NZ), F32),
            pltpu.VMEM((2, 9, 16, NZ), F32),
            pltpu.VMEM((2, 9, comps, 24, NZ), F32),
            pltpu.VMEM((2, 9, 16, NZ), F32),
            pltpu.VMEM((CX * CY, NZ), jnp.int32),
            pltpu.SMEM(visc_table.shape, F32),
            pltpu.VMEM(marker_cell.shape, jnp.int32),
            pltpu.VMEM(marker_frac.shape, F32),
            pltpu.VMEM(multiplier.shape, F32),
            pltpu.VMEM((comps, CX * CY, NZ), F32),
            pltpu.VMEM(pair_sphere.shape, jnp.int32),
            pltpu.VMEM(pair_partner.shape, jnp.int32),
            pltpu.VMEM(pair_normal.shape, F32),
            pltpu.VMEM(pair_gap.shape, F32),
            pltpu.VMEM(contact_force.shape, F32),
            pltpu.VMEM((PAD, 2 * NZ), F32),
            pltpu.VMEM((SPH, ROWS, 2 * NZ), F32),
            pltpu.VMEM((SPH, ROWS, NZ), F32),
            pltpu.VMEM((CHUNKS, ROWS, CHUNK), F32),
            pltpu.VMEM((CHUNKS, 2 * NZ, CHUNK), BF16),
            pltpu.VMEM((PAD, NZ), F32),
            pltpu.VMEM((2 * PAD, 2 * NZ), BF16),
            pltpu.VMEM((comps, SPH, MARK), F32),
            pltpu.VMEM((2, 8, NZ), F32),
            pltpu.VMEM((2, 9, 8, NZ), F32),
            pltpu.VMEM((8, 32), F32),
            pltpu.VMEM((1, 32), F32),
            pltpu.VMEM((comps, CX * CY, NZ), F32),
            pltpu.VMEM(multiplier.shape, F32),
            pltpu.VMEM(contact_force.shape, F32),
            pltpu.SemaphoreType.DMA((15,)),
            pltpu.SemaphoreType.DMA((6, 9)),
            pltpu.SemaphoreType.DMA((6, 9)),
        ],
        compiler_params=pltpu.CompilerParams(
            collective_id=0, has_side_effects=True, vmem_limit_bytes=63 * 1024 * 1024
        ),
    )(
        velocity.reshape(comps, CX * CY, NZ), force.reshape(comps, CX * CY, NZ), visc_class.reshape(CX * CY, NZ),
        visc_table, multiplier, marker_cell, marker_frac, pair_sphere, pair_partner, pair_normal, pair_gap, contact_force,
    )
    out = pl.pallas_call(
        hand_over,
        out_shape=out_shape,
        in_specs=[hbm] * 3,
        out_specs=(hbm, hbm, hbm),
        scratch_shapes=[pltpu.SemaphoreType.DMA((3,))],
        compiler_params=pltpu.CompilerParams(vmem_limit_bytes=63 * 1024 * 1024),
    )(*out)
    return (out[0].reshape(comps, CX, CY, NZ), out[1], out[2])


def solution(mesh):
    in_specs = (
        P(None, "wide", "narrow", None),
        P(None, "wide", "narrow", None),
        P("wide", "narrow", None),
        P(),
        P(None, ("wide", "narrow"), None),
        P(("wide", "narrow"), None),
        P(None, ("wide", "narrow"), None),
        P(("wide", "narrow")),
        P(("wide", "narrow")),
        P(None, ("wide", "narrow")),
        P(("wide", "narrow")),
        P(("wide", "narrow")),
    )
    out_specs = (
        P(None, "wide", "narrow", None),
        P(None, ("wide", "narrow"), None),
        P(("wide", "narrow")),
    )
    return jax.shard_map(local, mesh=mesh, in_specs=in_specs, out_specs=out_specs, check_vma=False)
```

```python
import jax
import jax.numpy as jnp
from jax import lax
from jax.experimental import pallas as pl
from jax.experimental.pallas import tpu as pltpu
from jax.sharding import PartitionSpec as P

ITERS = 2
MESH = pl.DeviceIdType.MESH
F32 = jnp.float32
BF16 = jnp.bfloat16

CX, CY, NZ = 8, 8, 128
SPH, MARK = 2, 2048
CHUNK = 256
PER_SPHERE = MARK // CHUNK
CHUNKS = SPH * PER_SPHERE
ROWS = 88
PAD = 272
EXT = 13 * 16
HALO0, FORCE0, HALO1, FORCE1, RIGID0, RIGID1 = range(6)
OTHERS = [0, 1, 2, 3, 5, 6, 7, 8]


def row(x, y):
    return (x + 2) * 16 + y % 16


def span(direction):
    return (0, 1, 2) if direction == 1 else (6, 7)


def split(value):
    high = value.astype(BF16)
    low = (value - high.astype(F32)).astype(BF16)
    return high, low


def body(
    vel_hbm, force_hbm, class_hbm, table_hbm, mult_hbm, cell_hbm, frac_hbm, sphere_hbm, partner_hbm, normal_hbm, gap_hbm,
    contact_hbm, vel_out, mult_out, contact_out,
    own, ext, pack, halo_in, halo_diag, halo_diag_in, coef, rhs, grid, grid_pack, grid_diag, grid_in, diag_in,
    visc_class, table, cell, frac, mult, force, pair_sphere, pair_partner, normal, gap, contact,
    acc, share_acc, share, plane_w, depth_w, stack, left, mult_mid, rigid, rigid_in, normal8, contact_mid,
    load_sem, send_sem, recv_sem,
):
    wide, narrow = lax.axis_index("wide"), lax.axis_index("narrow")
    n_wide, n_narrow = lax.axis_size("wide"), lax.axis_size("narrow")

    def neighbour(d):
        dx, dy = d // 3 - 1, d % 3 - 1
        return (lax.rem(wide + dx + n_wide, n_wide), lax.rem(narrow + dy + n_narrow, n_narrow))

    def exists(d):
        dx, dy = d // 3 - 1, d % 3 - 1
        return (wide + dx >= 0) & (wide + dx < n_wide) & (narrow + dy >= 0) & (narrow + dy < n_narrow)

    barrier = pltpu.get_barrier_semaphore()
    for d in OTHERS:
        @pl.when(exists(d))
        def greet(d=d):
            pl.semaphore_signal(barrier, inc=1, device_id=neighbour(d), device_id_type=MESH)
    across = jnp.where(wide > 0, 1, 0) + jnp.where(wide < n_wide - 1, 1, 0) + 1
    along = jnp.where(narrow > 0, 1, 0) + jnp.where(narrow < n_narrow - 1, 1, 0) + 1

    loads = [
        pltpu.make_async_copy(src, dst, load_sem.at[k])
        for k, (src, dst) in enumerate((
            (class_hbm, visc_class), (table_hbm, table), (vel_hbm, own.at[0, 0:3]), (cell_hbm, cell), (frac_hbm, frac),
            (mult_hbm, mult), (force_hbm, force), (sphere_hbm, pair_sphere), (partner_hbm, pair_partner),
            (normal_hbm, normal), (gap_hbm, gap), (contact_hbm, contact),
        ))
    ]
    for load in loads:
        load.start()

    def transfer(kind, s, src, dst):
        return pltpu.make_async_remote_copy(
            src_ref=src, dst_ref=dst, send_sem=send_sem.at[kind, s], recv_sem=recv_sem.at[kind, s],
            device_id=neighbour(8 - s), device_id_type=MESH,
        )

    def halo_copies(turn):
        fields = 4 if turn == 0 else 3
        copies = []
        for s in OTHERS:
            dx, dy = s // 3 - 1, s % 3 - 1
            if dx != 0 and dy != 0:
                count = fields * len(span(dx)) * len(span(dy))
                rows = (count + 7) // 8 * 8
                copies.append(transfer(HALO0 if turn == 0 else HALO1, s, halo_diag.at[turn, s, 0:rows], halo_diag_in.at[turn, s, 0:rows]))
                continue
            if dy == 0:
                rows = 24 if dx == 1 else 16
                first = 0 if dx == 1 else 48
                src = own.at[turn, 0:fields, first:first + rows]
            else:
                rows = 24 if dy == 1 else 16
                src = pack.at[turn, 0 if dy == 1 else 1, 0:fields, 0:rows]
            copies.append(transfer(HALO0 if turn == 0 else HALO1, s, src, halo_in.at[turn, s, 0:fields, 0:rows]))
        return copies

    def force_copies(turn):
        copies = []
        for s in OTHERS:
            dx, dy = s // 3 - 1, s % 3 - 1
            if dx != 0 and dy != 0:
                src, dst = grid_diag.at[turn, s], diag_in.at[turn, s]
            elif dy == 0:
                start = 0 if dx == 1 else 64
                src, dst = grid.at[turn, :, start:start + 24], grid_in.at[turn, s]
            else:
                src, dst = grid_pack.at[turn, 0 if dy == 1 else 1], grid_in.at[turn, s]
            copies.append(transfer(FORCE0 if turn == 0 else FORCE1, s, src, dst))
        return copies

    def rigid_copies(turn):
        return [
            transfer(RIGID0 if turn == 0 else RIGID1, s, rigid.at[turn], rigid_in.at[turn, s]) for s in OTHERS
        ]

    def start(copies):
        for s, copy in zip(OTHERS, copies):
            @pl.when(exists(8 - s))
            def go(copy=copy):
                copy.start()

    def arrive(copies):
        for s, copy in zip(OTHERS, copies):
            @pl.when(exists(s))
            def go(copy=copy):
                copy.wait_recv()

    def leave(copies):
        for s, copy in zip(OTHERS, copies):
            @pl.when(exists(8 - s))
            def go(copy=copy):
                copy.wait_send()

    def received(s, value):
        return jnp.where(exists(s), value, F32(0.0))

    def pack_halo(turn):
        fields = 4 if turn == 0 else 3
        for f in range(fields):
            for j in range(3):
                pack[turn, 0, f, 8 * j:8 * j + 8, :] = own[turn, f, pl.ds(j, 8, stride=8), :]
            for j in range(2):
                pack[turn, 1, f, 8 * j:8 * j + 8, :] = own[turn, f, pl.ds(6 + j, 8, stride=8), :]

        for s in (0, 2, 6, 8):
            xs, ys = span(s // 3 - 1), span(s % 3 - 1)
            for f in range(fields):
                for j, y in enumerate(ys):
                    at = (f * len(ys) + j) * len(xs)
                    halo_diag[turn, s, at:at + len(xs), :] = own[turn, f, pl.ds(xs[0] * 8 + y, len(xs), stride=8), :]

    def unpack_halo(turn):
        fields = 4 if turn == 0 else 3
        for f in range(fields):
            for i in range(3):
                ext[turn, f, pl.ds(row(8 + i, 0), 8), :] = received(7, halo_in[turn, 7, f, 8 * i:8 * i + 8, :])
            for i in range(2):
                ext[turn, f, pl.ds(row(i - 2, 0), 8), :] = received(1, halo_in[turn, 1, f, 8 * i:8 * i + 8, :])
            for j in range(3):
                ext[turn, f, pl.ds(row(0, 8 + j), 8, stride=16), :] = received(5, halo_in[turn, 5, f, 8 * j:8 * j + 8, :])
            for j in range(2):
                ext[turn, f, pl.ds(row(0, j - 2), 8, stride=16), :] = received(3, halo_in[turn, 3, f, 8 * j:8 * j + 8, :])
            for s in (0, 2, 6, 8):
                xs, ys = span(s // 3 - 1), span(s % 3 - 1)
                x0 = 8 if s // 3 == 2 else -2
                y0 = 8 if s % 3 == 2 else -2
                for j in range(len(ys)):
                    at = (f * len(ys) + j) * len(xs)
                    ext[turn, f, pl.ds(row(x0, y0 + j), len(xs), stride=16), :] = received(
                        s, halo_diag_in[turn, s, at:at + len(xs), :]
                    )

    for load in loads[0:3]:
        load.wait()
    classes = visc_class[...]
    mu = jnp.where(classes == 0, table[0], jnp.where(classes == 1, table[1], jnp.where(classes == 2, table[2], table[3])))
    mu = jnp.where((classes >= 0) & (classes <= 3), mu, F32(0.0))
    own[0, 3, :, :] = mu
    for f in range(4):
        for x in range(8):
            ext[0, f, pl.ds(row(x, 0), 8), :] = own[0, f, 8 * x:8 * x + 8, :]
    pack_halo(0)

    pl.semaphore_wait(barrier, across * along - 1)
    start(halo_copies(0))

    for load in loads[3:]:
        load.wait()
    acc[...] = jnp.zeros_like(acc)
    share_acc[...] = jnp.zeros_like(share_acc)

    def add_spread(lhs, depth):
        high, low = split(lhs)
        dims = (((1,), (1,)), ((), ()))
        return lax.dot_general(high, depth, dims, preferred_element_type=F32) + lax.dot_general(
            low, depth, dims, preferred_element_type=F32
        )

    def setup(n, carry):
        s, k = n // PER_SPHERE, n % PER_SPHERE
        lanes = pl.ds(pl.multiple_of(k * CHUNK, CHUNK), CHUNK)
        spot = cell[pl.ds(s, 1), lanes]
        cell_x, cell_y, cell_z = spot >> 10, (spot >> 7) & 7, spot & 127
        frac_x, frac_y, frac_z = (frac[a, pl.ds(s, 1), lanes] for a in range(3))
        gap_z = lax.broadcasted_iota(jnp.int32, (NZ, CHUNK), 0) - cell_z
        depth = jnp.where(gap_z == 0, 1.0 - frac_z, jnp.where(gap_z == 1, frac_z, F32(0.0)))
        depth_high, depth_low = split(depth)
        depth_w[n, 0:NZ, :] = depth_high
        depth_w[n, NZ:2 * NZ, :] = depth_low
        next_x = jnp.where(wide == n_wide - 1, F32(0.0), frac_x)
        next_y = jnp.where(narrow == n_narrow - 1, F32(0.0), frac_y)
        gap_8 = lax.broadcasted_iota(jnp.int32, (8, CHUNK), 0)
        weight_y = jnp.where(gap_8 == cell_y, 1.0 - frac_y, jnp.where(gap_8 == cell_y + 1, frac_y, F32(0.0)))
        weight_x = jnp.where(gap_8 == cell_x, 1.0 - frac_x, jnp.where(gap_8 == cell_x + 1, frac_x, F32(0.0)))
        last_x = jnp.where(cell_x == 7, next_x, F32(0.0))
        last_y = jnp.where(cell_y == 7, next_y, F32(0.0))
        tiles = [weight_x * last_y]
        for x in range(8):
            tiles.append(weight_x[x:x + 1] * weight_y)
        tiles.append(last_x * weight_y)
        corner = jnp.where(gap_8 == 0, weight_x[7:8], jnp.where(gap_8 == 1, last_x, F32(0.0))) * last_y
        tiles.append(corner)
        weight = jnp.concatenate(tiles, axis=0)
        plane_w[n] = weight
        lhs = [weight * (0.25 * mult[c, pl.ds(s, 1), lanes]) for c in range(3)]
        result = add_spread(jnp.concatenate(lhs + [weight], axis=0), depth_w[n])
        acc[0:264, :] += result[0:264]
        share_acc[s] += result[264:352]
        return carry

    lax.fori_loop(0, CHUNKS, setup, 0, unroll=8)
    for s in range(SPH):
        share[s] = (share_acc[s, :, 0:NZ] + share_acc[s, :, NZ:2 * NZ]) * F32(1.0 / MARK)

    def send_force(turn):
        for c in range(3):
            base = c * ROWS
            for t in range(11):
                part = acc[base + 8 * t:base + 8 * t + 8, 0:NZ] + acc[base + 8 * t:base + 8 * t + 8, NZ:2 * NZ]
                if 1 <= t <= 8:
                    part = part + force[c, 8 * t - 8:8 * t, :]
                grid[turn, c, 8 * t:8 * t + 8, :] = part
            for j in range(2):
                grid_pack[turn, 0, c, 8 * j:8 * j + 8, :] = grid[turn, c, pl.ds(8 + j, 8, stride=8), :]
            grid_pack[turn, 0, c, 16:24, :] = grid[turn, c, 72:80, :]
            grid_pack[turn, 1, c, 0:8, :] = grid[turn, c, pl.ds(15, 8, stride=8), :]
            grid_pack[turn, 1, c, 8:16, :] = grid[turn, c, 0:8, :]
            grid_pack[turn, 1, c, 16:17, :] = grid[turn, c, 79:80, :]
            grid_pack[turn, 1, c, 17:18, :] = grid[turn, c, 81:82, :]
            for s in (0, 2, 6, 8):
                dx, dy = s // 3 - 1, s % 3 - 1
                first = 8 if dx == 1 else 64
                for j in range(2):
                    if dy == 1:
                        rows = grid[turn, c, pl.ds(first + j, 2, stride=8), :]
                    elif j == 0:
                        rows = grid[turn, c, pl.ds(first + 7, 2, stride=8), :]
                    else:
                        at = 0 if dx == 1 else 80
                        rows = grid[turn, c, at:at + 2, :]
                    grid_diag[turn, s, 4 * c + 2 * j:4 * c + 2 * j + 2, :] = rows
        start(force_copies(turn))

    send_force(0)

    halos = halo_copies(0)
    arrive(halos)
    unpack_halo(0)
    row_id = lax.broadcasted_iota(jnp.int32, (16, NZ), 0)
    lane_id = lax.broadcasted_iota(jnp.int32, (16, NZ), 1)
    y_id = narrow * CY + jnp.where(row_id > 11, row_id - 16, row_id)

    def in_y(y):
        return (y >= 0) & (y < n_narrow * CY)

    def coefficients(i, carry):
        def viscosity(shift):
            x = wide * CX + i - 1 + shift
            inside = in_y(y_id) & (x >= 0) & (x < n_wide * CX)
            at = pl.multiple_of((i + 1 + shift) * 16, 16)
            return jnp.where(inside, ext[0, 3, pl.ds(at, 16), :], F32(0.0))

        mid = viscosity(0)
        x = wide * CX + i - 1
        around = [
            viscosity(-1),
            viscosity(1),
            jnp.where(in_y(y_id - 1), pltpu.roll(mid, 1, 0), F32(0.0)),
            jnp.where(in_y(y_id + 1), pltpu.roll(mid, 15, 0), F32(0.0)),
            jnp.where(lane_id == 0, F32(0.0), pltpu.roll(mid, 1, 1)),
            jnp.where(lane_id == NZ - 1, F32(0.0), pltpu.roll(mid, NZ - 1, 1)),
        ]
        valid = [
            (x - 1 >= 0) & (lane_id >= 0),
            (x + 1 < n_wide * CX) & (lane_id >= 0),
            in_y(y_id - 1),
            in_y(y_id + 1),
            lane_id > 0,
            lane_id < NZ - 1,
        ]
        faces = [0.5 * (mid + other) for other in around]
        diagonal = 1.0 + faces[0] + faces[1] + faces[2] + faces[3] + faces[4] + faces[5]
        inside = in_y(y_id) & (x >= 0) & (x < n_wide * CX)
        inverse = jnp.where(inside, 1.0 / diagonal, F32(0.0))
        at = pl.ds(pl.multiple_of(i * 16, 16), 16)
        for a in range(6):
            coef[a, at, :] = jnp.where(valid[a], faces[a] * inverse, F32(0.0))
        coef[6, at, :] = inverse
        return carry

    lax.fori_loop(0, 11, coefficients, 0, unroll=True)
    rhs[...] = jnp.zeros_like(rhs)
    stack[...] = jnp.zeros_like(stack)
    normal8[...] = jnp.zeros_like(normal8)
    normal8[0:3, :] = normal[...]
    normal8[4:7, :] = normal[...]

    sphere_row = lax.broadcasted_iota(jnp.int32, (8, 32), 0) // 4
    pair_s = pair_sphere[...].reshape(1, 32)
    pair_q = pair_partner[...].reshape(1, 32)
    contact_mid[...] = contact[...].reshape(1, 32)
    pair_gap = gap[...].reshape(1, 32)

    def gather_force(turn):
        arrive(force_copies(turn))
        for c in range(3):
            def add(x, y, n, stride, value):
                at = pl.ds(row(x, y), n, stride=stride) if stride != 1 else pl.ds(row(x, y), n)
                rhs[turn, c, at, :] += value

            for x in range(9):
                rhs[turn, c, pl.ds(row(x, 0), 8), :] = grid[turn, c, 8 + 8 * x:16 + 8 * x, :]
            rhs[turn, c, pl.ds(row(0, 8), 8, stride=16), :] = grid[turn, c, 0:8, :]
            rhs[turn, c, pl.ds(row(8, 8), 1), :] = grid[turn, c, 81:82, :]
            add(8, 0, 8, 1, received(7, grid_in[turn, 7, c, 8:16, :]))
            add(9, 0, 8, 1, received(7, grid_in[turn, 7, c, 16:24, :]))
            add(8, 8, 2, 16, received(7, grid_in[turn, 7, c, 0:2, :]))
            add(-1, 0, 8, 1, received(1, grid_in[turn, 1, c, 0:8, :]))
            add(0, 0, 8, 1, received(1, grid_in[turn, 1, c, 8:16, :]))
            add(-1, 8, 2, 16, received(1, grid_in[turn, 1, c, 16:18, :]))
            for s, low in ((5, 8), (3, -1)):
                for j in range(2):
                    add(0, low + j, 8, 16, received(s, grid_in[turn, s, c, 8 * j:8 * j + 8, :]))
                    add(8, low + j, 1, 1, received(s, grid_in[turn, s, c, 16 + j:17 + j, :]))
            for s in (0, 2, 6, 8):
                x = 8 if s // 3 == 2 else -1
                y = 8 if s % 3 == 2 else -1
                for j in range(2):
                    add(x, y + j, 2, 16, received(s, diag_in[turn, s, 4 * c + 2 * j:4 * c + 2 * j + 2, :]))

    def sweep(source, target, first, count, turn):
        def one(i, carry):
            at = pl.ds(pl.multiple_of(i * 16, 16), 16)
            factors = [coef[a, at, :] for a in range(7)]
            for c in range(3):
                def load(shift):
                    return source[c, pl.ds(pl.multiple_of((i + 1 + shift) * 16, 16), 16), :]

                mid = load(0)
                value = factors[6] * rhs[turn, c, pl.ds(pl.multiple_of((i + 1) * 16, 16), 16), :]
                value += factors[0] * load(-1)
                value += factors[1] * load(1)
                value += factors[2] * pltpu.roll(mid, 1, 0)
                value += factors[3] * pltpu.roll(mid, 15, 0)
                value += factors[4] * pltpu.roll(mid, 1, 1)
                value += factors[5] * pltpu.roll(mid, NZ - 1, 1)
                target[c, pl.ds(pl.multiple_of((i + 1) * 16, 16), 16), :] = value
            return carry

        lax.fori_loop(first, first + count, one, 0, unroll=True)

    def update_contact(turn):
        quarter = pair_q // 2
        partner = jnp.zeros((8, 32), F32)
        for q in range(9):
            if q == 4:
                tile = rigid[turn, :, 0:32]
            else:
                tile = received(q, rigid_in[turn, q, :, 0:32])
            partner = jnp.where(quarter == q, tile, partner)
        closing8 = jnp.where(sphere_row == pair_q - 2 * quarter, partner, F32(0.0)) - jnp.where(
            sphere_row == pair_s, rigid[turn, :, 0:32], F32(0.0)
        )
        closing = jnp.sum(normal8[...] * closing8, axis=0, keepdims=True)
        return jnp.maximum(F32(0.0), contact_mid[...] - 0.5 * (pair_gap + closing))

    for turn in range(ITERS):
        last = turn == ITERS - 1
        if turn > 0:
            arrive(halo_copies(turn))
            unpack_halo(turn)
        gather_force(turn)
        middle = ext.at[2]
        sweep(ext.at[turn], middle, 0, 11, turn)
        sweep(middle, ext.at[3], 1, 9, turn)
        done = ext.at[3]
        for c in range(3):
            for x in range(9):
                tile = done[c, pl.ds(row(x, 0), 8), :]
                stack[c * ROWS + 8 + 8 * x:c * ROWS + 16 + 8 * x, :] = tile
                if x < 8:
                    if last:
                        vel_out[c, 8 * x:8 * x + 8, :] = tile
                    else:
                        own[turn + 1, c, 8 * x:8 * x + 8, :] = tile
                        ext[turn + 1, c, pl.ds(row(x, 0), 8), :] = tile
            stack[c * ROWS:c * ROWS + 8, :] = done[c, pl.ds(row(0, 8), 8, stride=16), :]
            stack[c * ROWS + 81:c * ROWS + 82, :] = done[c, pl.ds(row(8, 8), 1), :]
        if not last:
            pack_halo(turn + 1)
            start(halo_copies(turn + 1))
        if turn > 0:
            arrive(rigid_copies(turn - 1))
            contact_mid[...] = update_contact(turn - 1)
        sums = jnp.zeros((8, NZ), F32)
        row8 = lax.broadcasted_iota(jnp.int32, (8, NZ), 0)
        for s in range(SPH):
            for c in range(3):
                part = jnp.sum(share[s] * stack[c * ROWS:(c + 1) * ROWS, :], axis=0, keepdims=True)
                sums = jnp.where(row8 == 4 * s + c, part, sums)
        push = jnp.where(sphere_row == pair_s, normal8[...] * contact_mid[...], F32(0.0))
        speed = jnp.sum(sums, axis=1, keepdims=True) + 0.5 * jnp.sum(push, axis=1, keepdims=True)
        rigid[turn] = jnp.broadcast_to(speed, (8, NZ))
        start(rigid_copies(turn))
        high, low = split(stack[...])
        left[0:PAD, 0:NZ] = high
        left[0:PAD, NZ:2 * NZ] = high
        left[PAD:2 * PAD, 0:NZ] = low
        left[PAD:2 * PAD, NZ:2 * NZ] = low
        if not last:
            acc[...] = jnp.zeros_like(acc)
        source = mult if turn == 0 else mult_mid

        def markers(n, carry):
            s, k = n // PER_SPHERE, n % PER_SPHERE
            lanes = pl.ds(pl.multiple_of(k * CHUNK, CHUNK), CHUNK)
            weight = plane_w[n]
            sampled = jnp.dot(left[0:PAD], depth_w[n], preferred_element_type=F32) + jnp.dot(left[PAD:2 * PAD], depth_w[n], preferred_element_type=F32)
            lhs = []
            for c in range(3):
                rows = slice(c * ROWS, (c + 1) * ROWS)
                low_rows = slice(PAD + c * ROWS, PAD + (c + 1) * ROWS)
                read = jnp.sum(sampled[rows] * weight, axis=0, keepdims=True)
                speed = rigid[turn, pl.ds(4 * s + c, 1), 0:1]
                new = source[c, pl.ds(s, 1), lanes] + 0.5 * (speed - read)
                if last:
                    mult_out[c, pl.ds(s, 1), lanes] = new
                else:
                    mult_mid[c, pl.ds(s, 1), lanes] = new
                    lhs.append(weight * (0.25 * new))
            if not last:
                lhs.append(jnp.zeros((8, CHUNK), F32))
                acc[...] += add_spread(jnp.concatenate(lhs, axis=0), depth_w[n])
            return carry

        lax.fori_loop(0, CHUNKS, markers, 0, unroll=8)
        if not last:
            send_force(turn + 1)
    arrive(rigid_copies(ITERS - 1))
    contact_out[...] = update_contact(ITERS - 1).reshape(32)
    for turn in range(ITERS):
        leave(halo_copies(turn))
        leave(force_copies(turn))
        leave(rigid_copies(turn))


def hand_over(vel, mult, contact, vel_out, mult_out, contact_out, sem):
    copies = [
        pltpu.make_async_copy(src, dst, sem.at[k])
        for k, (src, dst) in enumerate(((vel, vel_out), (mult, mult_out), (contact, contact_out)))
    ]
    for copy in copies:
        copy.start()
    for copy in copies:
        copy.wait()


def local(
    velocity, force, visc_class, visc_table, multiplier, marker_cell, marker_frac,
    pair_sphere, pair_partner, pair_normal, pair_gap, contact_force,
):
    comps = 3
    vmem = pl.BlockSpec(memory_space=pltpu.VMEM)
    hbm = pl.BlockSpec(memory_space=pltpu.MemorySpace.HBM)
    out_shape = (
        jax.ShapeDtypeStruct((comps, CX * CY, NZ), F32),
        jax.ShapeDtypeStruct(multiplier.shape, F32),
        jax.ShapeDtypeStruct(contact_force.shape, F32),
    )
    out = pl.pallas_call(
        body,
        out_shape=tuple(pltpu.VMEM(shape.shape, shape.dtype) for shape in out_shape),
        in_specs=[hbm] * 12,
        out_specs=(vmem, vmem, vmem),
        scratch_shapes=[
            pltpu.VMEM((2, 4, CX * CY, NZ), F32),
            pltpu.VMEM((4, 4, EXT, NZ), F32),
            pltpu.VMEM((2, 2, 4, 24, NZ), F32),
            pltpu.VMEM((2, 9, 4, 24, NZ), F32),
            pltpu.VMEM((2, 9, 40, NZ), F32),
            pltpu.VMEM((2, 9, 40, NZ), F32),
            pltpu.VMEM((7, 11 * 16, NZ), F32),
            pltpu.VMEM((2, comps, EXT, NZ), F32),
            pltpu.VMEM((2, comps, ROWS, NZ), F32),
            pltpu.VMEM((2, 2, comps, 24, NZ), F32),
            pltpu.VMEM((2, 9, 16, NZ), F32),
            pltpu.VMEM((2, 9, comps, 24, NZ), F32),
            pltpu.VMEM((2, 9, 16, NZ), F32),
            pltpu.VMEM((CX * CY, NZ), jnp.int32),
            pltpu.SMEM(visc_table.shape, F32),
            pltpu.VMEM(marker_cell.shape, jnp.int32),
            pltpu.VMEM(marker_frac.shape, F32),
            pltpu.VMEM(multiplier.shape, F32),
            pltpu.VMEM((comps, CX * CY, NZ), F32),
            pltpu.VMEM(pair_sphere.shape, jnp.int32),
            pltpu.VMEM(pair_partner.shape, jnp.int32),
            pltpu.VMEM(pair_normal.shape, F32),
            pltpu.VMEM(pair_gap.shape, F32),
            pltpu.VMEM(contact_force.shape, F32),
            pltpu.VMEM((PAD, 2 * NZ), F32),
            pltpu.VMEM((SPH, ROWS, 2 * NZ), F32),
            pltpu.VMEM((SPH, ROWS, NZ), F32),
            pltpu.VMEM((CHUNKS, ROWS, CHUNK), F32),
            pltpu.VMEM((CHUNKS, 2 * NZ, CHUNK), BF16),
            pltpu.VMEM((PAD, NZ), F32),
            pltpu.VMEM((2 * PAD, 2 * NZ), BF16),
            pltpu.VMEM((comps, SPH, MARK), F32),
            pltpu.VMEM((2, 8, NZ), F32),
            pltpu.VMEM((2, 9, 8, NZ), F32),
            pltpu.VMEM((8, 32), F32),
            pltpu.VMEM((1, 32), F32),
            pltpu.SemaphoreType.DMA((12,)),
            pltpu.SemaphoreType.DMA((6, 9)),
            pltpu.SemaphoreType.DMA((6, 9)),
        ],
        compiler_params=pltpu.CompilerParams(
            collective_id=0, has_side_effects=True, vmem_limit_bytes=62 * 1024 * 1024
        ),
    )(
        velocity.reshape(comps, CX * CY, NZ), force.reshape(comps, CX * CY, NZ), visc_class.reshape(CX * CY, NZ),
        visc_table, multiplier, marker_cell, marker_frac, pair_sphere, pair_partner, pair_normal, pair_gap, contact_force,
    )
    out = pl.pallas_call(
        hand_over,
        out_shape=out_shape,
        in_specs=[vmem] * 3,
        out_specs=(hbm, hbm, hbm),
        scratch_shapes=[pltpu.SemaphoreType.DMA((3,))],
        compiler_params=pltpu.CompilerParams(vmem_limit_bytes=1024 * 1024),
    )(*out)
    return (out[0].reshape(comps, CX, CY, NZ), out[1], out[2])


def solution(mesh):
    in_specs = (
        P(None, "wide", "narrow", None),
        P(None, "wide", "narrow", None),
        P("wide", "narrow", None),
        P(),
        P(None, ("wide", "narrow"), None),
        P(("wide", "narrow"), None),
        P(None, ("wide", "narrow"), None),
        P(("wide", "narrow")),
        P(("wide", "narrow")),
        P(None, ("wide", "narrow")),
        P(("wide", "narrow")),
        P(("wide", "narrow")),
    )
    out_specs = (
        P(None, "wide", "narrow", None),
        P(None, ("wide", "narrow"), None),
        P(("wide", "narrow")),
    )
    return jax.shard_map(local, mesh=mesh, in_specs=in_specs, out_specs=out_specs, check_vma=False)
```

```python
import jax
import jax.numpy as jnp
from jax import lax
from jax.experimental import pallas as pl
from jax.experimental.pallas import tpu as pltpu
from jax.sharding import PartitionSpec as P

ITERS = 2
MESH = pl.DeviceIdType.MESH
F32 = jnp.float32
BF16 = jnp.bfloat16

CX, CY, NZ = 8, 8, 128
SPH, MARK = 2, 2048
CHUNK = 256
PER_SPHERE = MARK // CHUNK
CHUNKS = SPH * PER_SPHERE
ROWS = 88
PAD = 272
EXT = 13 * 16
HALO0, FORCE0, HALO1, FORCE1, RIGID0, RIGID1 = range(6)
OTHERS = [3, 5, 0, 2, 6, 8, 1, 7]


def row(x, y):
    return (x + 2) * 16 + y % 16


def span(direction):
    return (0, 1, 2) if direction == 1 else (6, 7)


def split(value):
    high = value.astype(BF16)
    low = (value - high.astype(F32)).astype(BF16)
    return high, low


def body(
    vel_hbm, force_hbm, class_hbm, table_hbm, mult_hbm, cell_hbm, frac_hbm, sphere_hbm, partner_hbm, normal_hbm, gap_hbm,
    contact_hbm, vel_out, mult_out, contact_out,
    own, ext, pack, halo_in, halo_diag, halo_diag_in, coef, rhs, grid, grid_pack, grid_diag, grid_in, diag_in,
    visc_class, table, cell, frac, mult, force, pair_sphere, pair_partner, normal, gap, contact,
    acc, share_acc, share, plane_w, depth_w, stack, left, mult_mid, rigid, rigid_in, normal8, contact_mid,
    load_sem, send_sem, recv_sem,
):
    wide, narrow = lax.axis_index("wide"), lax.axis_index("narrow")
    n_wide, n_narrow = lax.axis_size("wide"), lax.axis_size("narrow")

    def neighbour(d):
        dx, dy = d // 3 - 1, d % 3 - 1
        return (lax.rem(wide + dx + n_wide, n_wide), lax.rem(narrow + dy + n_narrow, n_narrow))

    def exists(d):
        dx, dy = d // 3 - 1, d % 3 - 1
        return (wide + dx >= 0) & (wide + dx < n_wide) & (narrow + dy >= 0) & (narrow + dy < n_narrow)

    barrier = pltpu.get_barrier_semaphore()
    for d in OTHERS:
        @pl.when(exists(d))
        def greet(d=d):
            pl.semaphore_signal(barrier, inc=1, device_id=neighbour(d), device_id_type=MESH)
    across = jnp.where(wide > 0, 1, 0) + jnp.where(wide < n_wide - 1, 1, 0) + 1
    along = jnp.where(narrow > 0, 1, 0) + jnp.where(narrow < n_narrow - 1, 1, 0) + 1

    loads = [
        pltpu.make_async_copy(src, dst, load_sem.at[k])
        for k, (src, dst) in enumerate((
            (class_hbm, visc_class), (table_hbm, table), (vel_hbm, own.at[0, 0:3]), (cell_hbm, cell), (frac_hbm, frac),
            (mult_hbm, mult), (force_hbm, force), (sphere_hbm, pair_sphere), (partner_hbm, pair_partner),
            (normal_hbm, normal), (gap_hbm, gap), (contact_hbm, contact),
        ))
    ]
    for load in loads:
        load.start()

    def transfer(kind, s, src, dst):
        return pltpu.make_async_remote_copy(
            src_ref=src, dst_ref=dst, send_sem=send_sem.at[kind, s], recv_sem=recv_sem.at[kind, s],
            device_id=neighbour(8 - s), device_id_type=MESH,
        )

    def halo_copies(turn):
        fields = 4 if turn == 0 else 3
        copies = []
        for s in OTHERS:
            dx, dy = s // 3 - 1, s % 3 - 1
            if dx != 0 and dy != 0:
                count = fields * len(span(dx)) * len(span(dy))
                rows = (count + 7) // 8 * 8
                copies.append(transfer(HALO0 if turn == 0 else HALO1, s, halo_diag.at[turn, s, 0:rows], halo_diag_in.at[turn, s, 0:rows]))
                continue
            if dy == 0:
                rows = 24 if dx == 1 else 16
                first = 0 if dx == 1 else 48
                src = own.at[turn, 0:fields, first:first + rows]
            else:
                rows = 24 if dy == 1 else 16
                src = pack.at[turn, 0 if dy == 1 else 1, 0:fields, 0:rows]
            copies.append(transfer(HALO0 if turn == 0 else HALO1, s, src, halo_in.at[turn, s, 0:fields, 0:rows]))
        return copies

    def force_copies(turn):
        copies = []
        for s in OTHERS:
            dx, dy = s // 3 - 1, s % 3 - 1
            if dx != 0 and dy != 0:
                src, dst = grid_diag.at[turn, s], diag_in.at[turn, s]
            else:
                src, dst = grid_pack.at[turn, s], grid_in.at[turn, s]
            copies.append(transfer(FORCE0 if turn == 0 else FORCE1, s, src, dst))
        return copies

    def rigid_copies(turn):
        return [
            transfer(RIGID0 if turn == 0 else RIGID1, s, rigid.at[turn], rigid_in.at[turn, s]) for s in OTHERS
        ]

    def start(copies):
        for s, copy in zip(OTHERS, copies):
            @pl.when(exists(8 - s))
            def go(copy=copy):
                copy.start()

    def arrive(copies):
        for s, copy in zip(OTHERS, copies):
            @pl.when(exists(s))
            def go(copy=copy):
                copy.wait_recv()

    def leave(copies):
        for s, copy in zip(OTHERS, copies):
            @pl.when(exists(8 - s))
            def go(copy=copy):
                copy.wait_send()

    def received(s, value):
        return jnp.where(exists(s), value, F32(0.0))

    def pack_halo(turn):
        fields = 4 if turn == 0 else 3
        for f in range(fields):
            for j in range(3):
                pack[turn, 0, f, 8 * j:8 * j + 8, :] = own[turn, f, pl.ds(j, 8, stride=8), :]
            for j in range(2):
                pack[turn, 1, f, 8 * j:8 * j + 8, :] = own[turn, f, pl.ds(6 + j, 8, stride=8), :]

        for s in (0, 2, 6, 8):
            xs, ys = span(s // 3 - 1), span(s % 3 - 1)
            for f in range(fields):
                for j, y in enumerate(ys):
                    at = (f * len(ys) + j) * len(xs)
                    halo_diag[turn, s, at:at + len(xs), :] = own[turn, f, pl.ds(xs[0] * 8 + y, len(xs), stride=8), :]

    def unpack_halo(turn):
        fields = 4 if turn == 0 else 3
        for f in range(fields):
            for i in range(3):
                ext[turn, f, pl.ds(row(8 + i, 0), 8), :] = received(7, halo_in[turn, 7, f, 8 * i:8 * i + 8, :])
            for i in range(2):
                ext[turn, f, pl.ds(row(i - 2, 0), 8), :] = received(1, halo_in[turn, 1, f, 8 * i:8 * i + 8, :])
            for j in range(3):
                ext[turn, f, pl.ds(row(0, 8 + j), 8, stride=16), :] = received(5, halo_in[turn, 5, f, 8 * j:8 * j + 8, :])
            for j in range(2):
                ext[turn, f, pl.ds(row(0, j - 2), 8, stride=16), :] = received(3, halo_in[turn, 3, f, 8 * j:8 * j + 8, :])
            for s in (0, 2, 6, 8):
                xs, ys = span(s // 3 - 1), span(s % 3 - 1)
                x0 = 8 if s // 3 == 2 else -2
                y0 = 8 if s % 3 == 2 else -2
                for j in range(len(ys)):
                    at = (f * len(ys) + j) * len(xs)
                    ext[turn, f, pl.ds(row(x0, y0 + j), len(xs), stride=16), :] = received(
                        s, halo_diag_in[turn, s, at:at + len(xs), :]
                    )

    for load in loads[0:3]:
        load.wait()
    classes = visc_class[...]
    mu = jnp.where(classes == 0, table[0], jnp.where(classes == 1, table[1], jnp.where(classes == 2, table[2], table[3])))
    mu = jnp.where((classes >= 0) & (classes <= 3), mu, F32(0.0))
    own[0, 3, :, :] = mu
    for f in range(4):
        for x in range(8):
            ext[0, f, pl.ds(row(x, 0), 8), :] = own[0, f, 8 * x:8 * x + 8, :]
    pack_halo(0)

    for load in loads[3:]:
        load.wait()
    acc[...] = jnp.zeros_like(acc)
    share_acc[...] = jnp.zeros_like(share_acc)

    def add_spread(lhs, depth):
        high, low = split(lhs)
        dims = (((1,), (1,)), ((), ()))
        return lax.dot_general(high, depth, dims, preferred_element_type=F32) + lax.dot_general(
            low, depth, dims, preferred_element_type=F32
        )

    def setup(n, carry):
        s, k = n // PER_SPHERE, n % PER_SPHERE
        lanes = pl.ds(pl.multiple_of(k * CHUNK, CHUNK), CHUNK)
        spot = cell[pl.ds(s, 1), lanes]
        cell_x, cell_y, cell_z = spot >> 10, (spot >> 7) & 7, spot & 127
        frac_x, frac_y, frac_z = (frac[a, pl.ds(s, 1), lanes] for a in range(3))
        gap_z = lax.broadcasted_iota(jnp.int32, (NZ, CHUNK), 0) - cell_z
        depth = jnp.where(gap_z == 0, 1.0 - frac_z, jnp.where(gap_z == 1, frac_z, F32(0.0)))
        depth_high, depth_low = split(depth)
        depth_w[n, 0:NZ, :] = depth_high
        depth_w[n, NZ:2 * NZ, :] = depth_low
        next_x = jnp.where(wide == n_wide - 1, F32(0.0), frac_x)
        next_y = jnp.where(narrow == n_narrow - 1, F32(0.0), frac_y)
        gap_8 = lax.broadcasted_iota(jnp.int32, (8, CHUNK), 0)
        weight_y = jnp.where(gap_8 == cell_y, 1.0 - frac_y, jnp.where(gap_8 == cell_y + 1, frac_y, F32(0.0)))
        weight_x = jnp.where(gap_8 == cell_x, 1.0 - frac_x, jnp.where(gap_8 == cell_x + 1, frac_x, F32(0.0)))
        last_x = jnp.where(cell_x == 7, next_x, F32(0.0))
        last_y = jnp.where(cell_y == 7, next_y, F32(0.0))
        tiles = [weight_x * last_y]
        for x in range(8):
            tiles.append(weight_x[x:x + 1] * weight_y)
        tiles.append(last_x * weight_y)
        corner = jnp.where(gap_8 == 0, weight_x[7:8], jnp.where(gap_8 == 1, last_x, F32(0.0))) * last_y
        tiles.append(corner)
        weight = jnp.concatenate(tiles, axis=0)
        plane_w[n] = weight
        lhs = [weight * (0.25 * mult[c, pl.ds(s, 1), lanes]) for c in range(3)]
        lhs.append(jnp.zeros((8, CHUNK), F32))
        acc[...] += add_spread(jnp.concatenate(lhs, axis=0), depth_w[n])
        return carry

    def part(h, carry):
        lax.fori_loop(0, CHUNKS // 2, lambda k, none: setup(h * (CHUNKS // 2) + k, none), 0, unroll=8)

        @pl.when(h == 0)
        def meet():
            pl.semaphore_wait(barrier, across * along - 1)
            start(halo_copies(0))

        return carry

    lax.fori_loop(0, 2, part, 0)
    def send_force(turn):
        for c in range(3):
            base = c * ROWS
            for t in range(11):
                part = acc[base + 8 * t:base + 8 * t + 8, 0:NZ] + acc[base + 8 * t:base + 8 * t + 8, NZ:2 * NZ]
                if 1 <= t <= 8:
                    part = part + force[c, 8 * t - 8:8 * t, :]
                grid[turn, c, 8 * t:8 * t + 8, :] = part
        for s, tiles, extra in (
            (5, (pl.ds(8, 8, stride=8), pl.ds(9, 8, stride=8)), (72, 73)),
            (3, (pl.ds(15, 8, stride=8), pl.ds(0, 8)), (79, 81)),
        ):
            for c in range(3):
                for j in range(2):
                    grid_pack[turn, s, 16 * c + 8 * j:16 * c + 8 * j + 8, :] = grid[turn, c, tiles[j], :]
                    at = 48 + 2 * c + j
                    grid_pack[turn, s, at:at + 1, :] = grid[turn, c, extra[j]:extra[j] + 1, :]
        for c in range(3):
            for s in (0, 2, 6, 8):
                dx, dy = s // 3 - 1, s % 3 - 1
                first = 8 if dx == 1 else 64
                for j in range(2):
                    if dy == 1:
                        rows = grid[turn, c, pl.ds(first + j, 2, stride=8), :]
                    elif j == 0:
                        rows = grid[turn, c, pl.ds(first + 7, 2, stride=8), :]
                    else:
                        at = 0 if dx == 1 else 80
                        rows = grid[turn, c, at:at + 2, :]
                    grid_diag[turn, s, 4 * c + 2 * j:4 * c + 2 * j + 2, :] = rows
        for s, first, extra in ((7, 8, 0), (1, 64, 80)):
            for c in range(3):
                grid_pack[turn, s, 16 * c:16 * c + 16, :] = grid[turn, c, first:first + 16, :]
                grid_pack[turn, s, 48 + 2 * c:50 + 2 * c, :] = grid[turn, c, extra:extra + 2, :]
        start(force_copies(turn))

    send_force(0)

    def shares(n, carry):
        pad = jnp.zeros((8, CHUNK), F32)
        for s in range(SPH):
            lhs = jnp.concatenate([plane_w[s * PER_SPHERE + n], pad], axis=0)
            share_acc[s] += add_spread(lhs, depth_w[s * PER_SPHERE + n])
        return carry

    lax.fori_loop(0, PER_SPHERE, shares, 0, unroll=4)
    for s in range(SPH):
        share[s] = (share_acc[s, 0:ROWS, 0:NZ] + share_acc[s, 0:ROWS, NZ:2 * NZ]) * F32(1.0 / MARK)

    rhs[...] = jnp.zeros_like(rhs)
    stack[...] = jnp.zeros_like(stack)
    normal8[...] = jnp.zeros_like(normal8)
    normal8[0:3, :] = normal[...]
    normal8[4:7, :] = normal[...]

    sphere_row = lax.broadcasted_iota(jnp.int32, (8, 32), 0) // 4
    pair_s = pair_sphere[...].reshape(1, 32)
    pair_q = pair_partner[...].reshape(1, 32)
    contact_mid[...] = contact[...].reshape(1, 32)
    pair_gap = gap[...].reshape(1, 32)

    halos = halo_copies(0)
    arrive(halos)
    unpack_halo(0)
    row_id = lax.broadcasted_iota(jnp.int32, (16, NZ), 0)
    lane_id = lax.broadcasted_iota(jnp.int32, (16, NZ), 1)
    y_id = narrow * CY + jnp.where(row_id > 11, row_id - 16, row_id)

    def in_y(y):
        return (y >= 0) & (y < n_narrow * CY)

    def coefficients(i, carry):
        def viscosity(shift):
            x = wide * CX + i - 1 + shift
            inside = in_y(y_id) & (x >= 0) & (x < n_wide * CX)
            at = pl.multiple_of((i + 1 + shift) * 16, 16)
            return jnp.where(inside, ext[0, 3, pl.ds(at, 16), :], F32(0.0))

        mid = viscosity(0)
        x = wide * CX + i - 1
        around = [
            viscosity(-1),
            viscosity(1),
            jnp.where(in_y(y_id - 1), pltpu.roll(mid, 1, 0), F32(0.0)),
            jnp.where(in_y(y_id + 1), pltpu.roll(mid, 15, 0), F32(0.0)),
            jnp.where(lane_id == 0, F32(0.0), pltpu.roll(mid, 1, 1)),
            jnp.where(lane_id == NZ - 1, F32(0.0), pltpu.roll(mid, NZ - 1, 1)),
        ]
        valid = [
            (x - 1 >= 0) & (lane_id >= 0),
            (x + 1 < n_wide * CX) & (lane_id >= 0),
            in_y(y_id - 1),
            in_y(y_id + 1),
            lane_id > 0,
            lane_id < NZ - 1,
        ]
        faces = [0.5 * (mid + other) for other in around]
        diagonal = 1.0 + faces[0] + faces[1] + faces[2] + faces[3] + faces[4] + faces[5]
        inside = in_y(y_id) & (x >= 0) & (x < n_wide * CX)
        inverse = jnp.where(inside, 1.0 / diagonal, F32(0.0))
        at = pl.ds(pl.multiple_of(i * 16, 16), 16)
        for a in range(6):
            coef[a, at, :] = jnp.where(valid[a], faces[a] * inverse, F32(0.0))
        coef[6, at, :] = inverse
        return carry

    lax.fori_loop(0, 11, coefficients, 0, unroll=True)
    def own_force(turn):
        for c in range(3):
            for x in range(9):
                rhs[turn, c, pl.ds(row(x, 0), 8), :] = grid[turn, c, 8 + 8 * x:16 + 8 * x, :]
            rhs[turn, c, pl.ds(row(0, 8), 8, stride=16), :] = grid[turn, c, 0:8, :]
            rhs[turn, c, pl.ds(row(8, 8), 1), :] = grid[turn, c, 81:82, :]

    def gather_force(turn):
        def add(c, x, y, n, stride, s, value):
            at = pl.ds(row(x, y), n, stride=stride) if stride != 1 else pl.ds(row(x, y), n)
            rhs[turn, c, at, :] += received(s, value)

        copies = dict(zip(OTHERS, force_copies(turn)))
        for s in (7, 1, 5, 3, 0, 2, 6, 8):
            @pl.when(exists(s))
            def go(copy=copies[s]):
                copy.wait_recv()
            x = 8 if s // 3 == 2 else -1
            y = 8 if s % 3 == 2 else -1
            for c in range(3):
                if s in (1, 3, 5, 7):
                    tile = [grid_in[turn, s, 16 * c + 8 * j:16 * c + 8 * j + 8, :] for j in range(2)]
                    extra = grid_in[turn, s, 48 + 2 * c:50 + 2 * c, :]
                if s in (1, 7):
                    add(c, x, 0, 8, 1, s, tile[0])
                    add(c, x + 1, 0, 8, 1, s, tile[1])
                    add(c, x, 8, 2, 16, s, extra)
                elif s in (3, 5):
                    for j in range(2):
                        add(c, 0, y + j, 8, 16, s, tile[j])
                        add(c, 8, y + j, 1, 1, s, extra[j:j + 1])
                else:
                    for j in range(2):
                        at = 4 * c + 2 * j
                        add(c, x, y + j, 2, 16, s, diag_in[turn, s, at:at + 2, :])

    def neighbours(source, c, i, factors):
        def load(shift):
            return source[c, pl.ds(pl.multiple_of((i + 1 + shift) * 16, 16), 16), :]

        mid = load(0)
        value = factors[0] * load(-1) + factors[1] * load(1)
        value += factors[2] * pltpu.roll(mid, 1, 0) + factors[3] * pltpu.roll(mid, 15, 0)
        return value + (factors[4] * pltpu.roll(mid, 1, 1) + factors[5] * pltpu.roll(mid, NZ - 1, 1))

    def tiles(i):
        return pl.ds(pl.multiple_of(i * 16, 16), 16), pl.ds(pl.multiple_of((i + 1) * 16, 16), 16)

    def first_sweep(source, target):
        def one(i, carry):
            at, to = tiles(i)
            factors = [coef[a, at, :] for a in range(6)]
            for c in range(3):
                target[c, to, :] = neighbours(source, c, i, factors)
            return carry

        lax.fori_loop(0, 11, one, 0, unroll=True)

    def add_force(target, turn):
        def one(i, carry):
            at, to = tiles(i)
            inverse = coef[6, at, :]
            for c in range(3):
                value = inverse * rhs[turn, c, to, :]
                rhs[turn, c, to, :] = value
                target[c, to, :] += value
            return carry

        lax.fori_loop(0, 11, one, 0, unroll=True)

    def second_sweep(source, target, turn):
        def one(i, carry):
            at, to = tiles(i)
            factors = [coef[a, at, :] for a in range(6)]
            for c in range(3):
                target[c, to, :] = rhs[turn, c, to, :] + neighbours(source, c, i, factors)
            return carry

        lax.fori_loop(1, 10, one, 0, unroll=True)

    def update_contact(turn):
        quarter = pair_q // 2
        partner = jnp.zeros((8, 32), F32)
        for q in range(9):
            if q == 4:
                tile = rigid[turn, :, 0:32]
            else:
                tile = received(q, rigid_in[turn, q, :, 0:32])
            partner = jnp.where(quarter == q, tile, partner)
        closing8 = jnp.where(sphere_row == pair_q - 2 * quarter, partner, F32(0.0)) - jnp.where(
            sphere_row == pair_s, rigid[turn, :, 0:32], F32(0.0)
        )
        closing = jnp.sum(normal8[...] * closing8, axis=0, keepdims=True)
        return jnp.maximum(F32(0.0), contact_mid[...] - 0.5 * (pair_gap + closing))

    for turn in range(ITERS):
        last = turn == ITERS - 1
        if turn > 0:
            arrive(halo_copies(turn))
            unpack_halo(turn)
        own_force(turn)
        middle, done = ext.at[2], ext.at[3]
        first_sweep(ext.at[turn], middle)
        if turn > 0:
            arrive(rigid_copies(turn - 1))
            contact_mid[...] = update_contact(turn - 1)
        push = jnp.where(sphere_row == pair_s, normal8[...] * contact_mid[...], F32(0.0))
        push_sum = 0.5 * jnp.sum(push, axis=1, keepdims=True)
        gather_force(turn)
        add_force(middle, turn)
        second_sweep(middle, done, turn)
        for c in range(3):
            for x in range(9):
                tile = done[c, pl.ds(row(x, 0), 8), :]
                stack[c * ROWS + 8 + 8 * x:c * ROWS + 16 + 8 * x, :] = tile
                if x < 8:
                    if last:
                        vel_out[c, 8 * x:8 * x + 8, :] = tile
                    else:
                        own[turn + 1, c, 8 * x:8 * x + 8, :] = tile
                        ext[turn + 1, c, pl.ds(row(x, 0), 8), :] = tile
            stack[c * ROWS:c * ROWS + 8, :] = done[c, pl.ds(row(0, 8), 8, stride=16), :]
            stack[c * ROWS + 81:c * ROWS + 82, :] = done[c, pl.ds(row(8, 8), 1), :]
        sums = jnp.zeros((8, NZ), F32)
        row8 = lax.broadcasted_iota(jnp.int32, (8, NZ), 0)
        for s in range(SPH):
            for c in range(3):
                part = jnp.sum(share[s] * stack[c * ROWS:(c + 1) * ROWS, :], axis=0, keepdims=True)
                sums = jnp.where(row8 == 4 * s + c, part, sums)
        speed = jnp.sum(sums, axis=1, keepdims=True) + push_sum
        rigid[turn] = jnp.broadcast_to(speed, (8, NZ))
        if not last:
            pack_halo(turn + 1)
            start(halo_copies(turn + 1))
        start(rigid_copies(turn))
        high, low = split(stack[...])
        left[0:PAD, 0:NZ] = high
        left[0:PAD, NZ:2 * NZ] = high
        left[PAD:2 * PAD, 0:NZ] = low
        left[PAD:2 * PAD, NZ:2 * NZ] = low
        if not last:
            acc[...] = jnp.zeros_like(acc)
        source = mult if turn == 0 else mult_mid

        def markers(n, carry):
            s, k = n // PER_SPHERE, n % PER_SPHERE
            lanes = pl.ds(pl.multiple_of(k * CHUNK, CHUNK), CHUNK)
            weight = plane_w[n]
            sampled = jnp.dot(left[0:PAD], depth_w[n], preferred_element_type=F32) + jnp.dot(left[PAD:2 * PAD], depth_w[n], preferred_element_type=F32)
            lhs = []
            for c in range(3):
                rows = slice(c * ROWS, (c + 1) * ROWS)
                low_rows = slice(PAD + c * ROWS, PAD + (c + 1) * ROWS)
                read = jnp.sum(sampled[rows] * weight, axis=0, keepdims=True)
                speed = rigid[turn, pl.ds(4 * s + c, 1), 0:1]
                new = source[c, pl.ds(s, 1), lanes] + 0.5 * (speed - read)
                if last:
                    mult_out[c, pl.ds(s, 1), lanes] = new
                else:
                    mult_mid[c, pl.ds(s, 1), lanes] = new
                    lhs.append(weight * (0.25 * new))
            if not last:
                lhs.append(jnp.zeros((8, CHUNK), F32))
                acc[...] += add_spread(jnp.concatenate(lhs, axis=0), depth_w[n])
            return carry

        lax.fori_loop(0, CHUNKS, markers, 0, unroll=8)
        if not last:
            send_force(turn + 1)
    for turn in range(ITERS):
        leave(halo_copies(turn))
        leave(force_copies(turn))
    leave(rigid_copies(0))
    arrive(rigid_copies(ITERS - 1))
    contact_out[...] = update_contact(ITERS - 1).reshape(32)
    leave(rigid_copies(ITERS - 1))


def hand_over(vel, mult, contact, vel_out, mult_out, contact_out, sem):
    copies = [
        pltpu.make_async_copy(src, dst, sem.at[k])
        for k, (src, dst) in enumerate(((vel, vel_out), (mult, mult_out), (contact, contact_out)))
    ]
    for copy in copies:
        copy.start()
    for copy in copies:
        copy.wait()


def local(
    velocity, force, visc_class, visc_table, multiplier, marker_cell, marker_frac,
    pair_sphere, pair_partner, pair_normal, pair_gap, contact_force,
):
    comps = 3
    vmem = pl.BlockSpec(memory_space=pltpu.VMEM)
    hbm = pl.BlockSpec(memory_space=pltpu.MemorySpace.HBM)
    out_shape = (
        jax.ShapeDtypeStruct((comps, CX * CY, NZ), F32),
        jax.ShapeDtypeStruct(multiplier.shape, F32),
        jax.ShapeDtypeStruct(contact_force.shape, F32),
    )
    out = pl.pallas_call(
        body,
        out_shape=tuple(pltpu.VMEM(shape.shape, shape.dtype) for shape in out_shape),
        in_specs=[hbm] * 12,
        out_specs=(vmem, vmem, vmem),
        scratch_shapes=[
            pltpu.VMEM((2, 4, CX * CY, NZ), F32),
            pltpu.VMEM((4, 4, EXT, NZ), F32),
            pltpu.VMEM((2, 2, 4, 24, NZ), F32),
            pltpu.VMEM((2, 9, 4, 24, NZ), F32),
            pltpu.VMEM((2, 9, 40, NZ), F32),
            pltpu.VMEM((2, 9, 40, NZ), F32),
            pltpu.VMEM((7, 11 * 16, NZ), F32),
            pltpu.VMEM((2, comps, EXT, NZ), F32),
            pltpu.VMEM((2, comps, ROWS, NZ), F32),
            pltpu.VMEM((2, 9, 56, NZ), F32),
            pltpu.VMEM((2, 9, 16, NZ), F32),
            pltpu.VMEM((2, 9, 56, NZ), F32),
            pltpu.VMEM((2, 9, 16, NZ), F32),
            pltpu.VMEM((CX * CY, NZ), jnp.int32),
            pltpu.SMEM(visc_table.shape, F32),
            pltpu.VMEM(marker_cell.shape, jnp.int32),
            pltpu.VMEM(marker_frac.shape, F32),
            pltpu.VMEM(multiplier.shape, F32),
            pltpu.VMEM((comps, CX * CY, NZ), F32),
            pltpu.VMEM(pair_sphere.shape, jnp.int32),
            pltpu.VMEM(pair_partner.shape, jnp.int32),
            pltpu.VMEM(pair_normal.shape, F32),
            pltpu.VMEM(pair_gap.shape, F32),
            pltpu.VMEM(contact_force.shape, F32),
            pltpu.VMEM((PAD, 2 * NZ), F32),
            pltpu.VMEM((SPH, 96, 2 * NZ), F32),
            pltpu.VMEM((SPH, ROWS, NZ), F32),
            pltpu.VMEM((CHUNKS, ROWS, CHUNK), F32),
            pltpu.VMEM((CHUNKS, 2 * NZ, CHUNK), BF16),
            pltpu.VMEM((PAD, NZ), F32),
            pltpu.VMEM((2 * PAD, 2 * NZ), BF16),
            pltpu.VMEM((comps, SPH, MARK), F32),
            pltpu.VMEM((2, 8, NZ), F32),
            pltpu.VMEM((2, 9, 8, NZ), F32),
            pltpu.VMEM((8, 32), F32),
            pltpu.VMEM((1, 32), F32),
            pltpu.SemaphoreType.DMA((12,)),
            pltpu.SemaphoreType.DMA((6, 9)),
            pltpu.SemaphoreType.DMA((6, 9)),
        ],
        compiler_params=pltpu.CompilerParams(
            collective_id=0, has_side_effects=True, vmem_limit_bytes=62 * 1024 * 1024
        ),
    )(
        velocity.reshape(comps, CX * CY, NZ), force.reshape(comps, CX * CY, NZ), visc_class.reshape(CX * CY, NZ),
        visc_table, multiplier, marker_cell, marker_frac, pair_sphere, pair_partner, pair_normal, pair_gap, contact_force,
    )
    out = pl.pallas_call(
        hand_over,
        out_shape=out_shape,
        in_specs=[vmem] * 3,
        out_specs=(hbm, hbm, hbm),
        scratch_shapes=[pltpu.SemaphoreType.DMA((3,))],
        compiler_params=pltpu.CompilerParams(vmem_limit_bytes=1024 * 1024),
    )(*out)
    return (out[0].reshape(comps, CX, CY, NZ), out[1], out[2])


def solution(mesh):
    in_specs = (
        P(None, "wide", "narrow", None),
        P(None, "wide", "narrow", None),
        P("wide", "narrow", None),
        P(),
        P(None, ("wide", "narrow"), None),
        P(("wide", "narrow"), None),
        P(None, ("wide", "narrow"), None),
        P(("wide", "narrow")),
        P(("wide", "narrow")),
        P(None, ("wide", "narrow")),
        P(("wide", "narrow")),
        P(("wide", "narrow")),
    )
    out_specs = (
        P(None, "wide", "narrow", None),
        P(None, ("wide", "narrow"), None),
        P(("wide", "narrow")),
    )
    return jax.shard_map(local, mesh=mesh, in_specs=in_specs, out_specs=out_specs, check_vma=False)
```

```python
import jax
import jax.numpy as jnp
from jax import lax
from jax.experimental import pallas as pl
from jax.experimental.pallas import tpu as pltpu
from jax.sharding import PartitionSpec as P

ITERS = 2
MESH = pl.DeviceIdType.MESH
F32 = jnp.float32
BF16 = jnp.bfloat16

CX, CY, NZ = 8, 8, 128
SPH, MARK = 2, 2048
CHUNK = 256
PER_SPHERE = MARK // CHUNK
CHUNKS = SPH * PER_SPHERE
ROWS = 88
PAD = 272
EXT = 13 * 16
HALO0, FORCE0, HALO1, FORCE1, RIGID0, REACH = range(6)
OTHERS = [3, 5, 0, 2, 6, 8, 1, 7]
FAR = [(x, y) for x in range(-2, 3) for y in range(-2, 3) if (x, y) != (0, 0)]


def row(x, y):
    return (x + 2) * 16 + y % 16


def span(direction):
    return (0, 1, 2) if direction == 1 else (6, 7)


def split(value):
    high = value.astype(BF16)
    low = (value - high.astype(F32)).astype(BF16)
    return high, low


def body(
    vel_hbm, force_hbm, class_hbm, table_hbm, mult_hbm, cell_hbm, frac_hbm, sphere_hbm, partner_hbm, normal_hbm, gap_hbm,
    contact_hbm, vel_out, mult_out, contact_out,
    own, ext, pack, halo_in, halo_diag, halo_diag_in, coef, rhs, grid, grid_pack, grid_diag, grid_in, diag_in,
    visc_class, table, cell, frac, mult, force, pair_sphere, pair_partner, normal, gap, contact,
    acc, share_acc, share, plane_w, depth_w, stack, left, mult_mid, rigid, rigid_in, normal8, contact_mid,
    spot_w, once, reach, reach_pack, reach_in, table8, table_in, load_sem, send_sem, recv_sem, far_send, far_recv,
):
    wide, narrow = lax.axis_index("wide"), lax.axis_index("narrow")
    n_wide, n_narrow = lax.axis_size("wide"), lax.axis_size("narrow")

    def neighbour(d):
        dx, dy = d // 3 - 1, d % 3 - 1
        return (lax.rem(wide + dx + n_wide, n_wide), lax.rem(narrow + dy + n_narrow, n_narrow))

    def exists(d):
        dx, dy = d // 3 - 1, d % 3 - 1
        return (wide + dx >= 0) & (wide + dx < n_wide) & (narrow + dy >= 0) & (narrow + dy < n_narrow)

    barrier = pltpu.get_barrier_semaphore()
    for d in OTHERS:
        @pl.when(exists(d))
        def greet(d=d):
            pl.semaphore_signal(barrier, inc=1, device_id=neighbour(d), device_id_type=MESH)
    across = jnp.where(wide > 0, 1, 0) + jnp.where(wide < n_wide - 1, 1, 0) + 1
    along = jnp.where(narrow > 0, 1, 0) + jnp.where(narrow < n_narrow - 1, 1, 0) + 1

    loads = [
        pltpu.make_async_copy(src, dst, load_sem.at[k])
        for k, (src, dst) in enumerate((
            (class_hbm, visc_class), (table_hbm, table), (vel_hbm, own.at[0, 0:3]), (cell_hbm, cell), (frac_hbm, frac),
            (mult_hbm, mult), (force_hbm, force), (sphere_hbm, pair_sphere), (partner_hbm, pair_partner),
            (normal_hbm, normal), (gap_hbm, gap), (contact_hbm, contact),
        ))
    ]
    for load in loads:
        load.start()
    ext[0:2] = jnp.zeros((2, 4, EXT, NZ), F32)
    spot_w[...] = jnp.zeros_like(spot_w)

    def transfer(kind, s, src, dst):
        return pltpu.make_async_remote_copy(
            src_ref=src, dst_ref=dst, send_sem=send_sem.at[kind, s], recv_sem=recv_sem.at[kind, s],
            device_id=neighbour(8 - s), device_id_type=MESH,
        )

    def halo_copies(turn):
        fields = 4 if turn == 0 else 3
        copies = []
        for s in OTHERS:
            dx, dy = s // 3 - 1, s % 3 - 1
            if dx != 0 and dy != 0:
                count = fields * len(span(dx)) * len(span(dy))
                rows = (count + 7) // 8 * 8
                copies.append(transfer(HALO0 if turn == 0 else HALO1, s, halo_diag.at[turn, s, 0:rows], halo_diag_in.at[turn, s, 0:rows]))
                continue
            if dy == 0:
                rows = 24 if dx == 1 else 16
                first = 0 if dx == 1 else 48
                src = own.at[turn, 0:fields, first:first + rows]
            else:
                rows = 24 if dy == 1 else 16
                src = pack.at[turn, 0 if dy == 1 else 1, 0:fields, 0:rows]
            copies.append(transfer(HALO0 if turn == 0 else HALO1, s, src, halo_in.at[turn, s, 0:fields, 0:rows]))
        return copies

    def force_copies(turn):
        copies = []
        for s in OTHERS:
            dx, dy = s // 3 - 1, s % 3 - 1
            if dx != 0 and dy != 0:
                src, dst = grid_diag.at[turn, s], diag_in.at[turn, s]
            else:
                src, dst = grid_pack.at[turn, s], grid_in.at[turn, s]
            copies.append(transfer(FORCE0 if turn == 0 else FORCE1, s, src, dst))
        return copies

    def rigid_copies():
        return [transfer(RIGID0, s, rigid.at[0], rigid_in.at[s]) for s in OTHERS]

    def reach_copies():
        copies = []
        for s in OTHERS:
            rows = 8 if s in (0, 2, 6, 8) else 40
            copies.append(transfer(REACH, s, reach_pack.at[8 - s, 0:rows], reach_in.at[s, 0:rows]))
        return copies

    def there(x, y):
        return (wide + x >= 0) & (wide + x < n_wide) & (narrow + y >= 0) & (narrow + y < n_narrow)

    def shift_copies():
        copies = []
        for x, y in FAR:
            n = (x + 2) * 5 + y + 2
            to = (lax.rem(wide - x + n_wide, n_wide), lax.rem(narrow - y + n_narrow, n_narrow))
            copies.append(pltpu.make_async_remote_copy(
                src_ref=table8, dst_ref=table_in.at[n], send_sem=far_send.at[n], recv_sem=far_recv.at[n],
                device_id=to, device_id_type=MESH,
            ))
        return copies

    def start(copies):
        for s, copy in zip(OTHERS, copies):
            @pl.when(exists(8 - s))
            def go(copy=copy):
                copy.start()

    def arrive(copies):
        for s, copy in zip(OTHERS, copies):
            @pl.when(exists(s))
            def go(copy=copy):
                copy.wait_recv()

    def leave(copies):
        for s, copy in zip(OTHERS, copies):
            @pl.when(exists(8 - s))
            def go(copy=copy):
                copy.wait_send()

    def received(s, value):
        return jnp.where(exists(s), value, F32(0.0))

    def pack_halo(turn):
        fields = 4 if turn == 0 else 3
        for f in range(fields):
            for j in range(3):
                pack[turn, 0, f, 8 * j:8 * j + 8, :] = own[turn, f, pl.ds(j, 8, stride=8), :]
            for j in range(2):
                pack[turn, 1, f, 8 * j:8 * j + 8, :] = own[turn, f, pl.ds(6 + j, 8, stride=8), :]

        for s in (0, 2, 6, 8):
            xs, ys = span(s // 3 - 1), span(s % 3 - 1)
            for f in range(fields):
                for j, y in enumerate(ys):
                    at = (f * len(ys) + j) * len(xs)
                    halo_diag[turn, s, at:at + len(xs), :] = own[turn, f, pl.ds(xs[0] * 8 + y, len(xs), stride=8), :]

    def unpack_halo(turn):
        fields = 4 if turn == 0 else 3
        for f in range(fields):
            for i in range(3):
                ext[turn, f, pl.ds(row(8 + i, 0), 8), :] = received(7, halo_in[turn, 7, f, 8 * i:8 * i + 8, :])
            for i in range(2):
                ext[turn, f, pl.ds(row(i - 2, 0), 8), :] = received(1, halo_in[turn, 1, f, 8 * i:8 * i + 8, :])
            for j in range(3):
                ext[turn, f, pl.ds(row(0, 8 + j), 8, stride=16), :] = received(5, halo_in[turn, 5, f, 8 * j:8 * j + 8, :])
            for j in range(2):
                ext[turn, f, pl.ds(row(0, j - 2), 8, stride=16), :] = received(3, halo_in[turn, 3, f, 8 * j:8 * j + 8, :])
            for s in (0, 2, 6, 8):
                xs, ys = span(s // 3 - 1), span(s % 3 - 1)
                x0 = 8 if s // 3 == 2 else -2
                y0 = 8 if s % 3 == 2 else -2
                for j in range(len(ys)):
                    at = (f * len(ys) + j) * len(xs)
                    ext[turn, f, pl.ds(row(x0, y0 + j), len(xs), stride=16), :] = received(
                        s, halo_diag_in[turn, s, at:at + len(xs), :]
                    )

    for load in loads[0:3]:
        load.wait()
    classes = visc_class[...]
    mu = jnp.where(classes == 0, table[0], jnp.where(classes == 1, table[1], jnp.where(classes == 2, table[2], table[3])))
    mu = jnp.where((classes >= 0) & (classes <= 3), mu, F32(0.0))
    own[0, 3, :, :] = mu
    for f in range(4):
        for x in range(8):
            ext[0, f, pl.ds(row(x, 0), 8), :] = own[0, f, 8 * x:8 * x + 8, :]
    pack_halo(0)

    for load in loads[3:]:
        load.wait()
    acc[...] = jnp.zeros_like(acc)
    share_acc[...] = jnp.zeros_like(share_acc)

    def add_spread(lhs, depth):
        high, low = split(lhs)
        dims = (((1,), (1,)), ((), ()))
        return lax.dot_general(high, depth, dims, preferred_element_type=F32) + lax.dot_general(
            low, depth, dims, preferred_element_type=F32
        )

    def setup(n, carry):
        s, k = n // PER_SPHERE, n % PER_SPHERE
        lanes = pl.ds(pl.multiple_of(k * CHUNK, CHUNK), CHUNK)
        spot = cell[pl.ds(s, 1), lanes]
        cell_x, cell_y, cell_z = spot >> 10, (spot >> 7) & 7, spot & 127
        frac_x, frac_y, frac_z = (frac[a, pl.ds(s, 1), lanes] for a in range(3))
        gap_z = lax.broadcasted_iota(jnp.int32, (NZ, CHUNK), 0) - cell_z
        depth = jnp.where(gap_z == 0, 1.0 - frac_z, jnp.where(gap_z == 1, frac_z, F32(0.0)))
        depth_high, depth_low = split(depth)
        depth_w[n, 0:NZ, :] = depth_high
        depth_w[n, NZ:2 * NZ, :] = depth_low
        next_x = jnp.where(wide == n_wide - 1, F32(0.0), frac_x)
        next_y = jnp.where(narrow == n_narrow - 1, F32(0.0), frac_y)
        gap_8 = lax.broadcasted_iota(jnp.int32, (8, CHUNK), 0)
        weight_y = jnp.where(gap_8 == cell_y, 1.0 - frac_y, jnp.where(gap_8 == cell_y + 1, frac_y, F32(0.0)))
        weight_x = jnp.where(gap_8 == cell_x, 1.0 - frac_x, jnp.where(gap_8 == cell_x + 1, frac_x, F32(0.0)))
        last_x = jnp.where(cell_x == 7, next_x, F32(0.0))
        last_y = jnp.where(cell_y == 7, next_y, F32(0.0))
        tiles = [weight_x * last_y]
        for x in range(8):
            tiles.append(weight_x[x:x + 1] * weight_y)
        tiles.append(last_x * weight_y)
        corner = jnp.where(gap_8 == 0, weight_x[7:8], jnp.where(gap_8 == 1, last_x, F32(0.0))) * last_y
        tiles.append(corner)
        weight = jnp.concatenate(tiles, axis=0)
        plane_w[n] = weight
        lhs = [weight * (0.25 * mult[c, pl.ds(s, 1), lanes]) for c in range(3)]
        lhs.append(jnp.zeros((8, CHUNK), F32))
        acc[...] += add_spread(jnp.concatenate(lhs, axis=0), depth_w[n])
        return carry

    def part(h, carry):
        lax.fori_loop(0, CHUNKS // 2, lambda k, none: setup(h * (CHUNKS // 2) + k, none), 0, unroll=8)

        @pl.when(h == 0)
        def meet():
            pl.semaphore_wait(barrier, across * along - 1)
            start(halo_copies(0))

        return carry

    lax.fori_loop(0, 2, part, 0)
    def send_force(turn):
        for c in range(3):
            base = c * ROWS
            for t in range(11):
                part = acc[base + 8 * t:base + 8 * t + 8, 0:NZ] + acc[base + 8 * t:base + 8 * t + 8, NZ:2 * NZ]
                if 1 <= t <= 8:
                    part = part + force[c, 8 * t - 8:8 * t, :]
                grid[turn, c, 8 * t:8 * t + 8, :] = part
        for s, tiles, extra in (
            (5, (pl.ds(8, 8, stride=8), pl.ds(9, 8, stride=8)), (72, 73)),
            (3, (pl.ds(15, 8, stride=8), pl.ds(0, 8)), (79, 81)),
        ):
            for c in range(3):
                for j in range(2):
                    grid_pack[turn, s, 16 * c + 8 * j:16 * c + 8 * j + 8, :] = grid[turn, c, tiles[j], :]
                    at = 48 + 2 * c + j
                    grid_pack[turn, s, at:at + 1, :] = grid[turn, c, extra[j]:extra[j] + 1, :]
        for c in range(3):
            for s in (0, 2, 6, 8):
                dx, dy = s // 3 - 1, s % 3 - 1
                first = 8 if dx == 1 else 64
                for j in range(2):
                    if dy == 1:
                        rows = grid[turn, c, pl.ds(first + j, 2, stride=8), :]
                    elif j == 0:
                        rows = grid[turn, c, pl.ds(first + 7, 2, stride=8), :]
                    else:
                        at = 0 if dx == 1 else 80
                        rows = grid[turn, c, at:at + 2, :]
                    grid_diag[turn, s, 4 * c + 2 * j:4 * c + 2 * j + 2, :] = rows
        for s, first, extra in ((7, 8, 0), (1, 64, 80)):
            for c in range(3):
                grid_pack[turn, s, 16 * c:16 * c + 16, :] = grid[turn, c, first:first + 16, :]
                grid_pack[turn, s, 48 + 2 * c:50 + 2 * c, :] = grid[turn, c, extra:extra + 2, :]
        start(force_copies(turn))

    send_force(0)

    def shares(n, carry):
        pad = jnp.zeros((8, CHUNK), F32)
        for s in range(SPH):
            lhs = jnp.concatenate([plane_w[s * PER_SPHERE + n], pad], axis=0)
            share_acc[s] += add_spread(lhs, depth_w[s * PER_SPHERE + n])
        return carry

    lax.fori_loop(0, PER_SPHERE, shares, 0, unroll=4)
    for s in range(SPH):
        share[s] = (share_acc[s, 0:ROWS, 0:NZ] + share_acc[s, 0:ROWS, NZ:2 * NZ]) * F32(1.0 / MARK)

    rhs[...] = jnp.zeros_like(rhs)
    stack[...] = jnp.zeros_like(stack)
    normal8[...] = jnp.zeros_like(normal8)
    normal8[0:3, :] = normal[...]
    normal8[4:7, :] = normal[...]

    sphere_row = lax.broadcasted_iota(jnp.int32, (8, 32), 0) // 4
    pair_s = pair_sphere[...].reshape(1, 32)
    pair_q = pair_partner[...].reshape(1, 32)
    contact_mid[...] = contact[...].reshape(1, 32)
    pair_gap = gap[...].reshape(1, 32)

    halos = halo_copies(0)
    arrive(halos)
    unpack_halo(0)
    row_id = lax.broadcasted_iota(jnp.int32, (16, NZ), 0)
    lane_id = lax.broadcasted_iota(jnp.int32, (16, NZ), 1)
    y_id = narrow * CY + jnp.where(row_id > 11, row_id - 16, row_id)

    def in_y(y):
        return (y >= 0) & (y < n_narrow * CY)

    def coefficients(i, carry):
        def viscosity(shift):
            x = wide * CX + i - 1 + shift
            inside = in_y(y_id) & (x >= 0) & (x < n_wide * CX)
            at = pl.multiple_of((i + 1 + shift) * 16, 16)
            return jnp.where(inside, ext[0, 3, pl.ds(at, 16), :], F32(0.0))

        mid = viscosity(0)
        x = wide * CX + i - 1
        around = [
            viscosity(-1),
            viscosity(1),
            jnp.where(in_y(y_id - 1), pltpu.roll(mid, 1, 0), F32(0.0)),
            jnp.where(in_y(y_id + 1), pltpu.roll(mid, 15, 0), F32(0.0)),
            jnp.where(lane_id == 0, F32(0.0), pltpu.roll(mid, 1, 1)),
            jnp.where(lane_id == NZ - 1, F32(0.0), pltpu.roll(mid, NZ - 1, 1)),
        ]
        valid = [
            (x - 1 >= 0) & (lane_id >= 0),
            (x + 1 < n_wide * CX) & (lane_id >= 0),
            in_y(y_id - 1),
            in_y(y_id + 1),
            lane_id > 0,
            lane_id < NZ - 1,
        ]
        faces = [0.5 * (mid + other) for other in around]
        diagonal = 1.0 + faces[0] + faces[1] + faces[2] + faces[3] + faces[4] + faces[5]
        inside = in_y(y_id) & (x >= 0) & (x < n_wide * CX)
        inverse = jnp.where(inside, 1.0 / diagonal, F32(0.0))
        at = pl.ds(pl.multiple_of(i * 16, 16), 16)
        for a in range(6):
            coef[a, at, :] = jnp.where(valid[a], faces[a] * inverse, F32(0.0))
        coef[6, at, :] = inverse
        return carry

    lax.fori_loop(0, 11, coefficients, 0, unroll=True)
    def own_force(turn):
        for c in range(3):
            for x in range(9):
                rhs[turn, c, pl.ds(row(x, 0), 8), :] = grid[turn, c, 8 + 8 * x:16 + 8 * x, :]
            rhs[turn, c, pl.ds(row(0, 8), 8, stride=16), :] = grid[turn, c, 0:8, :]
            rhs[turn, c, pl.ds(row(8, 8), 1), :] = grid[turn, c, 81:82, :]

    def gather_force(turn):
        def add(c, x, y, n, stride, s, value):
            at = pl.ds(row(x, y), n, stride=stride) if stride != 1 else pl.ds(row(x, y), n)
            rhs[turn, c, at, :] += received(s, value)

        copies = dict(zip(OTHERS, force_copies(turn)))
        for s in (7, 1, 5, 3, 0, 2, 6, 8):
            @pl.when(exists(s))
            def go(copy=copies[s]):
                copy.wait_recv()
            x = 8 if s // 3 == 2 else -1
            y = 8 if s % 3 == 2 else -1
            for c in range(3):
                if s in (1, 3, 5, 7):
                    tile = [grid_in[turn, s, 16 * c + 8 * j:16 * c + 8 * j + 8, :] for j in range(2)]
                    extra = grid_in[turn, s, 48 + 2 * c:50 + 2 * c, :]
                if s in (1, 7):
                    add(c, x, 0, 8, 1, s, tile[0])
                    add(c, x + 1, 0, 8, 1, s, tile[1])
                    add(c, x, 8, 2, 16, s, extra)
                elif s in (3, 5):
                    for j in range(2):
                        add(c, 0, y + j, 8, 16, s, tile[j])
                        add(c, 8, y + j, 1, 1, s, extra[j:j + 1])
                else:
                    for j in range(2):
                        at = 4 * c + 2 * j
                        add(c, x, y + j, 2, 16, s, diag_in[turn, s, at:at + 2, :])

    def neighbours(source, c, i, factors):
        def load(shift):
            return source[c, pl.ds(pl.multiple_of((i + 1 + shift) * 16, 16), 16), :]

        mid = load(0)
        value = factors[0] * load(-1) + factors[1] * load(1)
        value += factors[2] * pltpu.roll(mid, 1, 0) + factors[3] * pltpu.roll(mid, 15, 0)
        return value + (factors[4] * pltpu.roll(mid, 1, 1) + factors[5] * pltpu.roll(mid, NZ - 1, 1))

    def tiles(i):
        return pl.ds(pl.multiple_of(i * 16, 16), 16), pl.ds(pl.multiple_of((i + 1) * 16, 16), 16)

    def first_sweep(source, target):
        def one(i, carry):
            at, to = tiles(i)
            factors = [coef[a, at, :] for a in range(6)]
            for c in range(3):
                target[c, to, :] = neighbours(source, c, i, factors)
            return carry

        lax.fori_loop(0, 11, one, 0, unroll=True)

    def add_force(target, turn):
        def one(i, carry):
            at, to = tiles(i)
            inverse = coef[6, at, :]
            for c in range(3):
                value = inverse * rhs[turn, c, to, :]
                rhs[turn, c, to, :] = value
                target[c, to, :] += value
            return carry

        lax.fori_loop(0, 11, one, 0, unroll=True)

    def second_sweep(source, target, turn):
        def one(i, carry):
            at, to = tiles(i)
            factors = [coef[a, at, :] for a in range(6)]
            for c in range(3):
                target[c, to, :] = rhs[turn, c, to, :] + neighbours(source, c, i, factors)
            return carry

        lax.fori_loop(1, 10, one, 0, unroll=True)

    quarter = pair_q // 2

    def new_contact(partner, own_tile):
        closing8 = jnp.where(sphere_row == pair_q - 2 * quarter, partner, F32(0.0)) - jnp.where(
            sphere_row == pair_s, own_tile, F32(0.0)
        )
        closing = jnp.sum(normal8[...] * closing8, axis=0, keepdims=True)
        return jnp.maximum(F32(0.0), contact_mid[...] - 0.5 * (pair_gap + closing))

    def first_contact():
        partner = jnp.zeros((8, 32), F32)
        for q in range(9):
            tile = rigid[0, :, 0:32] if q == 4 else received(q, rigid_in[q, :, 0:32])
            partner = jnp.where(quarter == q, tile, partner)
        return new_contact(partner, rigid[0, :, 0:32])

    row8 = lax.broadcasted_iota(jnp.int32, (8, NZ), 0)
    lane8 = lax.broadcasted_iota(jnp.int32, (8, NZ), 1)

    def make_reach():
        for t in range(SPH):
            for x in range(9):
                spot_w[t, pl.ds(row(x, 0), 8), :] = share[t, 8 + 8 * x:16 + 8 * x, :]
            spot_w[t, pl.ds(row(0, 8), 8, stride=16), :] = share[t, 0:8, :]
            spot_w[t, pl.ds(row(8, 8), 1), :] = share[t, 81:82, :]
        for t in range(SPH):
            for i in range(11):
                to = pl.ds((i + 1) * 16, 16)
                mid = spot_w[t, to, :]
                value = jnp.zeros((16, NZ), F32)
                if i < 10:
                    value += coef[0, pl.ds((i + 1) * 16, 16), :] * spot_w[t, pl.ds((i + 2) * 16, 16), :]
                if i > 0:
                    value += coef[1, pl.ds((i - 1) * 16, 16), :] * spot_w[t, pl.ds(i * 16, 16), :]
                if 0 < i < 10:
                    at = pl.ds(i * 16, 16)
                    value += pltpu.roll(coef[2, at, :] * mid, 15, 0) + pltpu.roll(coef[3, at, :] * mid, 1, 0)
                    value += pltpu.roll(coef[4, at, :] * mid, NZ - 1, 1) + pltpu.roll(coef[5, at, :] * mid, 1, 1)
                once[t, to, :] = value
                reach[t, to, :] = coef[6, pl.ds(i * 16, 16), :] * (mid + value)
        for s in OTHERS:
            x = 8 if s // 3 == 2 else -1
            y = 8 if s % 3 == 2 else -1
            for t in range(SPH):
                for j in range(2):
                    if s in (1, 7):
                        reach_pack[s, 16 * t + 8 * j:16 * t + 8 * j + 8, :] = reach[t, pl.ds(row(x + j, 0), 8), :]
                    elif s in (3, 5):
                        reach_pack[s, 16 * t + 8 * j:16 * t + 8 * j + 8, :] = reach[t, pl.ds(row(0, y + j), 8, stride=16), :]
                        at = 32 + 2 * t + j
                        reach_pack[s, at:at + 1, :] = reach[t, pl.ds(row(8, y + j), 1), :]
                    else:
                        at = 4 * t + 2 * j
                        reach_pack[s, at:at + 2, :] = reach[t, pl.ds(row(x, y + j), 2, stride=16), :]
                if s in (1, 7):
                    reach_pack[s, 32 + 2 * t:34 + 2 * t, :] = reach[t, pl.ds(row(x, 8), 2, stride=16), :]

    def column(parts):
        tile = jnp.zeros((8, NZ), F32)
        for (t, c), part in parts.items():
            tile = jnp.where(row8 == 4 * t + c, jnp.sum(part, axis=0, keepdims=True), tile)
        return jnp.sum(tile, axis=1, keepdims=True)

    def given(turn):
        table = jnp.zeros((8, NZ), F32)
        for d in OTHERS:
            s = 8 - d
            parts = {}
            for t in range(SPH):
                for c in range(3):
                    if d in (0, 2, 6, 8):
                        part = reach_in[d, 4 * t:4 * t + 4, :] * grid_diag[turn, s, 4 * c:4 * c + 4, :]
                    else:
                        part = reach_in[d, 16 * t:16 * t + 8, :] * grid_pack[turn, s, 16 * c:16 * c + 8, :]
                        part += reach_in[d, 16 * t + 8:16 * t + 16, :] * grid_pack[turn, s, 16 * c + 8:16 * c + 16, :]
                        extra = reach_in[d, 32 + 2 * t:34 + 2 * t, :] * grid_pack[turn, s, 48 + 2 * c:50 + 2 * c, :]
                        part = jnp.concatenate([part, extra], axis=0)
                    parts[t, c] = part
            table = jnp.where(lane8 == d, received(d, column(parts)), table)
        return table

    def kept(turn, middle, push_sum):
        parts = {}
        for t in range(SPH):
            for c in range(3):
                total = jnp.zeros((16, NZ), F32)
                for i in range(11):
                    at = pl.ds((i + 1) * 16, 16)
                    total += reach[t, at, :] * rhs[turn, c, at, :] + once[t, at, :] * middle[c, at, :]
                parts[t, c] = total
        return column(parts) + push_sum

    def last_contact():
        lane_x, lane_y = lane8 // 3 - 1, lane8 - (lane8 // 3) * 3 - 1
        means = table8[...]
        for x, y in FAR + [(0, 0)]:
            n = (x + 2) * 5 + y + 2
            near = (lane8 < 9) & (abs(lane_x - x) <= 1) & (abs(lane_y - y) <= 1)
            if (x, y) == (0, 0):
                continue
            shifted = pltpu.roll(table_in[n], (3 * x + y) % NZ, 1)
            means += jnp.where(near & there(x, y), shifted, F32(0.0))
        partner = jnp.zeros((8, 32), F32)
        for q in range(9):
            partner = jnp.where(quarter == q, means[:, q:q + 1], partner)
        return new_contact(partner, rigid[1, :, 0:32])

    for turn in range(ITERS):
        last = turn == ITERS - 1
        if turn > 0:
            arrive(halo_copies(turn))
            unpack_halo(turn)
        own_force(turn)
        middle, done = ext.at[2], ext.at[3]
        first_sweep(ext.at[turn], middle)
        if turn > 0:
            arrive(rigid_copies())
            contact_mid[...] = first_contact()
        push = jnp.where(sphere_row == pair_s, normal8[...] * contact_mid[...], F32(0.0))
        push_sum = 0.5 * jnp.sum(push, axis=1, keepdims=True)
        if last:
            arrive(reach_copies())
            table8[...] = jnp.where(lane8 == 4, kept(turn, middle, push_sum), given(turn))
            for (x, y), copy in zip(FAR, shift_copies()):
                @pl.when(there(-x, -y))
                def go(copy=copy):
                    copy.start()
        else:
            make_reach()
            start(reach_copies())
        gather_force(turn)
        add_force(middle, turn)
        second_sweep(middle, done, turn)
        for c in range(3):
            for x in range(9):
                tile = done[c, pl.ds(row(x, 0), 8), :]
                stack[c * ROWS + 8 + 8 * x:c * ROWS + 16 + 8 * x, :] = tile
                if x < 8:
                    if last:
                        vel_out[c, 8 * x:8 * x + 8, :] = tile
                    else:
                        own[turn + 1, c, 8 * x:8 * x + 8, :] = tile
                        ext[turn + 1, c, pl.ds(row(x, 0), 8), :] = tile
            stack[c * ROWS:c * ROWS + 8, :] = done[c, pl.ds(row(0, 8), 8, stride=16), :]
            stack[c * ROWS + 81:c * ROWS + 82, :] = done[c, pl.ds(row(8, 8), 1), :]
        sums = jnp.zeros((8, NZ), F32)
        for s in range(SPH):
            for c in range(3):
                part = jnp.sum(share[s] * stack[c * ROWS:(c + 1) * ROWS, :], axis=0, keepdims=True)
                sums = jnp.where(row8 == 4 * s + c, part, sums)
        speed = jnp.sum(sums, axis=1, keepdims=True) + push_sum
        rigid[turn] = jnp.broadcast_to(speed, (8, NZ))
        if not last:
            pack_halo(turn + 1)
            start(halo_copies(turn + 1))
            start(rigid_copies())
        high, low = split(stack[...])
        left[0:PAD, 0:NZ] = high
        left[0:PAD, NZ:2 * NZ] = high
        left[PAD:2 * PAD, 0:NZ] = low
        left[PAD:2 * PAD, NZ:2 * NZ] = low
        if not last:
            acc[...] = jnp.zeros_like(acc)
        source = mult if turn == 0 else mult_mid

        def markers(n, carry):
            s, k = n // PER_SPHERE, n % PER_SPHERE
            lanes = pl.ds(pl.multiple_of(k * CHUNK, CHUNK), CHUNK)
            weight = plane_w[n]
            sampled = jnp.dot(left[0:PAD], depth_w[n], preferred_element_type=F32) + jnp.dot(left[PAD:2 * PAD], depth_w[n], preferred_element_type=F32)
            lhs = []
            for c in range(3):
                rows = slice(c * ROWS, (c + 1) * ROWS)
                low_rows = slice(PAD + c * ROWS, PAD + (c + 1) * ROWS)
                read = jnp.sum(sampled[rows] * weight, axis=0, keepdims=True)
                speed = rigid[turn, pl.ds(4 * s + c, 1), 0:1]
                new = source[c, pl.ds(s, 1), lanes] + 0.5 * (speed - read)
                if last:
                    mult_out[c, pl.ds(s, 1), lanes] = new
                else:
                    mult_mid[c, pl.ds(s, 1), lanes] = new
                    lhs.append(weight * (0.25 * new))
            if not last:
                lhs.append(jnp.zeros((8, CHUNK), F32))
                acc[...] += add_spread(jnp.concatenate(lhs, axis=0), depth_w[n])
            return carry

        lax.fori_loop(0, CHUNKS, markers, 0, unroll=8)
        if not last:
            send_force(turn + 1)
    for turn in range(ITERS):
        leave(halo_copies(turn))
        leave(force_copies(turn))
    leave(rigid_copies())
    leave(reach_copies())
    for (x, y), copy in zip(FAR, shift_copies()):
        @pl.when(there(-x, -y))
        def gone(copy=copy):
            copy.wait_send()

        @pl.when(there(x, y))
        def come(copy=copy):
            copy.wait_recv()
    contact_out[...] = last_contact().reshape(32)


def hand_over(vel, mult, contact, vel_out, mult_out, contact_out, sem):
    copies = [
        pltpu.make_async_copy(src, dst, sem.at[k])
        for k, (src, dst) in enumerate(((vel, vel_out), (mult, mult_out), (contact, contact_out)))
    ]
    for copy in copies:
        copy.start()
    for copy in copies:
        copy.wait()


def local(
    velocity, force, visc_class, visc_table, multiplier, marker_cell, marker_frac,
    pair_sphere, pair_partner, pair_normal, pair_gap, contact_force,
):
    comps = 3
    vmem = pl.BlockSpec(memory_space=pltpu.VMEM)
    hbm = pl.BlockSpec(memory_space=pltpu.MemorySpace.HBM)
    out_shape = (
        jax.ShapeDtypeStruct((comps, CX * CY, NZ), F32),
        jax.ShapeDtypeStruct(multiplier.shape, F32),
        jax.ShapeDtypeStruct(contact_force.shape, F32),
    )
    out = pl.pallas_call(
        body,
        out_shape=tuple(pltpu.VMEM(shape.shape, shape.dtype) for shape in out_shape),
        in_specs=[hbm] * 12,
        out_specs=(vmem, vmem, vmem),
        scratch_shapes=[
            pltpu.VMEM((2, 4, CX * CY, NZ), F32),
            pltpu.VMEM((4, 4, EXT, NZ), F32),
            pltpu.VMEM((2, 2, 4, 24, NZ), F32),
            pltpu.VMEM((2, 9, 4, 24, NZ), F32),
            pltpu.VMEM((2, 9, 40, NZ), F32),
            pltpu.VMEM((2, 9, 40, NZ), F32),
            pltpu.VMEM((7, 11 * 16, NZ), F32),
            pltpu.VMEM((2, comps, EXT, NZ), F32),
            pltpu.VMEM((2, comps, ROWS, NZ), F32),
            pltpu.VMEM((2, 9, 56, NZ), F32),
            pltpu.VMEM((2, 9, 16, NZ), F32),
            pltpu.VMEM((2, 9, 56, NZ), F32),
            pltpu.VMEM((2, 9, 16, NZ), F32),
            pltpu.VMEM((CX * CY, NZ), jnp.int32),
            pltpu.SMEM(visc_table.shape, F32),
            pltpu.VMEM(marker_cell.shape, jnp.int32),
            pltpu.VMEM(marker_frac.shape, F32),
            pltpu.VMEM(multiplier.shape, F32),
            pltpu.VMEM((comps, CX * CY, NZ), F32),
            pltpu.VMEM(pair_sphere.shape, jnp.int32),
            pltpu.VMEM(pair_partner.shape, jnp.int32),
            pltpu.VMEM(pair_normal.shape, F32),
            pltpu.VMEM(pair_gap.shape, F32),
            pltpu.VMEM(contact_force.shape, F32),
            pltpu.VMEM((PAD, 2 * NZ), F32),
            pltpu.VMEM((SPH, 96, 2 * NZ), F32),
            pltpu.VMEM((SPH, ROWS, NZ), F32),
            pltpu.VMEM((CHUNKS, ROWS, CHUNK), F32),
            pltpu.VMEM((CHUNKS, 2 * NZ, CHUNK), BF16),
            pltpu.VMEM((PAD, NZ), F32),
            pltpu.VMEM((2 * PAD, 2 * NZ), BF16),
            pltpu.VMEM((comps, SPH, MARK), F32),
            pltpu.VMEM((2, 8, NZ), F32),
            pltpu.VMEM((9, 8, NZ), F32),
            pltpu.VMEM((8, 32), F32),
            pltpu.VMEM((1, 32), F32),
            pltpu.VMEM((SPH, EXT, NZ), F32),
            pltpu.VMEM((SPH, EXT, NZ), F32),
            pltpu.VMEM((SPH, EXT, NZ), F32),
            pltpu.VMEM((9, 40, NZ), F32),
            pltpu.VMEM((9, 40, NZ), F32),
            pltpu.VMEM((8, NZ), F32),
            pltpu.VMEM((25, 8, NZ), F32),
            pltpu.SemaphoreType.DMA((12,)),
            pltpu.SemaphoreType.DMA((6, 9)),
            pltpu.SemaphoreType.DMA((6, 9)),
            pltpu.SemaphoreType.DMA((25,)),
            pltpu.SemaphoreType.DMA((25,)),
        ],
        compiler_params=pltpu.CompilerParams(
            collective_id=0, has_side_effects=True, vmem_limit_bytes=62 * 1024 * 1024
        ),
    )(
        velocity.reshape(comps, CX * CY, NZ), force.reshape(comps, CX * CY, NZ), visc_class.reshape(CX * CY, NZ),
        visc_table, multiplier, marker_cell, marker_frac, pair_sphere, pair_partner, pair_normal, pair_gap, contact_force,
    )
    out = pl.pallas_call(
        hand_over,
        out_shape=out_shape,
        in_specs=[vmem] * 3,
        out_specs=(hbm, hbm, hbm),
        scratch_shapes=[pltpu.SemaphoreType.DMA((3,))],
        compiler_params=pltpu.CompilerParams(vmem_limit_bytes=1024 * 1024),
    )(*out)
    return (out[0].reshape(comps, CX, CY, NZ), out[1], out[2])


def solution(mesh):
    in_specs = (
        P(None, "wide", "narrow", None),
        P(None, "wide", "narrow", None),
        P("wide", "narrow", None),
        P(),
        P(None, ("wide", "narrow"), None),
        P(("wide", "narrow"), None),
        P(None, ("wide", "narrow"), None),
        P(("wide", "narrow")),
        P(("wide", "narrow")),
        P(None, ("wide", "narrow")),
        P(("wide", "narrow")),
        P(("wide", "narrow")),
    )
    out_specs = (
        P(None, "wide", "narrow", None),
        P(None, ("wide", "narrow"), None),
        P(("wide", "narrow")),
    )
    return jax.shard_map(local, mesh=mesh, in_specs=in_specs, out_specs=out_specs, check_vma=False)
```

```python
import jax
import jax.numpy as jnp
from jax import lax
from jax.experimental import pallas as pl
from jax.experimental.pallas import tpu as pltpu
from jax.sharding import PartitionSpec as P

ITERS = 2
MESH = pl.DeviceIdType.MESH
F32 = jnp.float32
BF16 = jnp.bfloat16

CX, CY, NZ = 8, 8, 128
SPH, MARK = 2, 2048
CHUNK = 256
PER_SPHERE = MARK // CHUNK
CHUNKS = SPH * PER_SPHERE
ROWS = 88
PAD = 272
EXT = 13 * 16
HALO0, FORCE0, HALO1, FORCE1, RIGID0, REACH = range(6)
OTHERS = [0, 2, 6, 8, 3, 5, 1, 7]
FAR = [(x, y) for x in range(-2, 3) for y in range(-2, 3) if (x, y) != (0, 0)]


def row(x, y):
    return (x + 2) * 16 + y % 16


def span(direction):
    return (0, 1, 2) if direction == 1 else (6, 7)


def split(value):
    high = value.astype(BF16)
    low = (value - high.astype(F32)).astype(BF16)
    return high, low


def body(
    vel_hbm, force_hbm, class_hbm, table_hbm, mult_hbm, cell_hbm, frac_hbm, sphere_hbm, partner_hbm, normal_hbm, gap_hbm,
    contact_hbm, vel_out, mult_out, contact_out,
    own, ext, pack, halo_in, halo_diag, halo_diag_in, coef, rhs, grid, grid_pack, grid_diag, grid_in, diag_in,
    visc_class, table, cell, frac, mult, force, pair_sphere, pair_partner, normal, gap, contact,
    acc, share_acc, share, plane_w, depth_w, stack, left, mult_mid, rigid, rigid_in, normal8, contact_mid,
    spot_w, once, reach, reach_pack, reach_in, table8, table_in, load_sem, send_sem, recv_sem, far_send, far_recv,
):
    wide, narrow = lax.axis_index("wide"), lax.axis_index("narrow")
    n_wide, n_narrow = lax.axis_size("wide"), lax.axis_size("narrow")

    def neighbour(d):
        dx, dy = d // 3 - 1, d % 3 - 1
        return (lax.rem(wide + dx + n_wide, n_wide), lax.rem(narrow + dy + n_narrow, n_narrow))

    def exists(d):
        dx, dy = d // 3 - 1, d % 3 - 1
        return (wide + dx >= 0) & (wide + dx < n_wide) & (narrow + dy >= 0) & (narrow + dy < n_narrow)

    loads = [
        pltpu.make_async_copy(src, dst, load_sem.at[k])
        for k, (src, dst) in enumerate((
            (cell_hbm, cell), (frac_hbm, frac), (mult_hbm, mult), (class_hbm, visc_class), (table_hbm, table),
            (vel_hbm, own.at[0, 0:3]), (force_hbm, force), (sphere_hbm, pair_sphere), (partner_hbm, pair_partner),
            (normal_hbm, normal), (gap_hbm, gap), (contact_hbm, contact),
        ))
    ]
    for load in loads:
        load.start()

    barrier = pltpu.get_barrier_semaphore()
    for d in OTHERS:
        @pl.when(exists(d))
        def greet(d=d):
            pl.semaphore_signal(barrier, inc=1, device_id=neighbour(d), device_id_type=MESH)
    across = jnp.where(wide > 0, 1, 0) + jnp.where(wide < n_wide - 1, 1, 0) + 1
    along = jnp.where(narrow > 0, 1, 0) + jnp.where(narrow < n_narrow - 1, 1, 0) + 1

    ext[0:2] = jnp.zeros((2, 4, EXT, NZ), F32)
    spot_w[...] = jnp.zeros_like(spot_w)

    def transfer(kind, s, src, dst):
        return pltpu.make_async_remote_copy(
            src_ref=src, dst_ref=dst, send_sem=send_sem.at[kind, s], recv_sem=recv_sem.at[kind, s],
            device_id=neighbour(8 - s), device_id_type=MESH,
        )

    def halo_copies(turn):
        fields = 4 if turn == 0 else 3
        copies = []
        for s in OTHERS:
            dx, dy = s // 3 - 1, s % 3 - 1
            if dx != 0 and dy != 0:
                count = fields * len(span(dx)) * len(span(dy))
                rows = (count + 7) // 8 * 8
                copies.append(transfer(HALO0 if turn == 0 else HALO1, s, halo_diag.at[turn, s, 0:rows], halo_diag_in.at[turn, s, 0:rows]))
                continue
            if dy == 0:
                rows = 24 if dx == 1 else 16
                first = 0 if dx == 1 else 48
                src = own.at[turn, 0:fields, first:first + rows]
            else:
                rows = 24 if dy == 1 else 16
                src = pack.at[turn, 0 if dy == 1 else 1, 0:fields, 0:rows]
            copies.append(transfer(HALO0 if turn == 0 else HALO1, s, src, halo_in.at[turn, s, 0:fields, 0:rows]))
        return copies

    def force_copies(turn):
        copies = []
        for s in OTHERS:
            dx, dy = s // 3 - 1, s % 3 - 1
            if dx != 0 and dy != 0:
                src, dst = grid_diag.at[turn, s], diag_in.at[turn, s]
            else:
                src, dst = grid_pack.at[turn, s], grid_in.at[turn, s]
            copies.append(transfer(FORCE0 if turn == 0 else FORCE1, s, src, dst))
        return copies

    def rigid_copies():
        return [transfer(RIGID0, s, rigid.at[0], rigid_in.at[s]) for s in OTHERS]

    def reach_copies():
        copies = []
        for s in OTHERS:
            rows = 8 if s in (0, 2, 6, 8) else 40
            copies.append(transfer(REACH, s, reach_pack.at[8 - s, 0:rows], reach_in.at[s, 0:rows]))
        return copies

    def there(x, y):
        return (wide + x >= 0) & (wide + x < n_wide) & (narrow + y >= 0) & (narrow + y < n_narrow)

    def shift_copies():
        copies = []
        for x, y in FAR:
            n = (x + 2) * 5 + y + 2
            to = (lax.rem(wide - x + n_wide, n_wide), lax.rem(narrow - y + n_narrow, n_narrow))
            copies.append(pltpu.make_async_remote_copy(
                src_ref=table8, dst_ref=table_in.at[n], send_sem=far_send.at[n], recv_sem=far_recv.at[n],
                device_id=to, device_id_type=MESH,
            ))
        return copies

    def start(copies):
        for s, copy in zip(OTHERS, copies):
            @pl.when(exists(8 - s))
            def go(copy=copy):
                copy.start()

    def arrive(copies):
        for s, copy in zip(OTHERS, copies):
            @pl.when(exists(s))
            def go(copy=copy):
                copy.wait_recv()

    def leave(copies):
        for s, copy in zip(OTHERS, copies):
            @pl.when(exists(8 - s))
            def go(copy=copy):
                copy.wait_send()

    def received(s, value):
        return jnp.where(exists(s), value, F32(0.0))

    def pack_halo(turn):
        fields = 4 if turn == 0 else 3
        for f in range(fields):
            for j in range(3):
                pack[turn, 0, f, 8 * j:8 * j + 8, :] = own[turn, f, pl.ds(j, 8, stride=8), :]
            for j in range(2):
                pack[turn, 1, f, 8 * j:8 * j + 8, :] = own[turn, f, pl.ds(6 + j, 8, stride=8), :]

        for s in (0, 2, 6, 8):
            xs, ys = span(s // 3 - 1), span(s % 3 - 1)
            for f in range(fields):
                for j, y in enumerate(ys):
                    at = (f * len(ys) + j) * len(xs)
                    halo_diag[turn, s, at:at + len(xs), :] = own[turn, f, pl.ds(xs[0] * 8 + y, len(xs), stride=8), :]

    def unpack_halo(turn):
        fields = 4 if turn == 0 else 3
        for f in range(fields):
            for i in range(3):
                ext[turn, f, pl.ds(row(8 + i, 0), 8), :] = received(7, halo_in[turn, 7, f, 8 * i:8 * i + 8, :])
            for i in range(2):
                ext[turn, f, pl.ds(row(i - 2, 0), 8), :] = received(1, halo_in[turn, 1, f, 8 * i:8 * i + 8, :])
            for j in range(3):
                ext[turn, f, pl.ds(row(0, 8 + j), 8, stride=16), :] = received(5, halo_in[turn, 5, f, 8 * j:8 * j + 8, :])
            for j in range(2):
                ext[turn, f, pl.ds(row(0, j - 2), 8, stride=16), :] = received(3, halo_in[turn, 3, f, 8 * j:8 * j + 8, :])
            for s in (0, 2, 6, 8):
                xs, ys = span(s // 3 - 1), span(s % 3 - 1)
                x0 = 8 if s // 3 == 2 else -2
                y0 = 8 if s % 3 == 2 else -2
                for j in range(len(ys)):
                    at = (f * len(ys) + j) * len(xs)
                    ext[turn, f, pl.ds(row(x0, y0 + j), len(xs), stride=16), :] = received(
                        s, halo_diag_in[turn, s, at:at + len(xs), :]
                    )

    for load in loads[3:6]:
        load.wait()
    classes = visc_class[...]
    mu = jnp.where(classes == 0, table[0], jnp.where(classes == 1, table[1], jnp.where(classes == 2, table[2], table[3])))
    mu = jnp.where((classes >= 0) & (classes <= 3), mu, F32(0.0))
    own[0, 3, :, :] = mu
    for f in range(4):
        for x in range(8):
            ext[0, f, pl.ds(row(x, 0), 8), :] = own[0, f, 8 * x:8 * x + 8, :]
    pack_halo(0)

    for load in loads[0:3] + loads[6:]:
        load.wait()
    acc[...] = jnp.zeros_like(acc)
    share_acc[...] = jnp.zeros_like(share_acc)

    def add_spread(lhs, depth):
        high, low = split(lhs)
        dims = (((1,), (1,)), ((), ()))
        both = lax.dot_general(high, depth, dims, preferred_element_type=F32)
        rest = lax.dot_general(low, depth[0:NZ], dims, preferred_element_type=F32)
        return both[:, 0:NZ] + both[:, NZ:2 * NZ] + rest

    def setup(n, carry):
        s, k = n // PER_SPHERE, n % PER_SPHERE
        lanes = pl.ds(pl.multiple_of(k * CHUNK, CHUNK), CHUNK)
        spot = cell[pl.ds(s, 1), lanes]
        cell_x, cell_y, cell_z = spot >> 10, (spot >> 7) & 7, spot & 127
        frac_x, frac_y, frac_z = (frac[a, pl.ds(s, 1), lanes] for a in range(3))
        gap_z = lax.broadcasted_iota(jnp.int32, (NZ, CHUNK), 0) - cell_z
        depth = jnp.where(gap_z == 0, 1.0 - frac_z, jnp.where(gap_z == 1, frac_z, F32(0.0)))
        depth_high, depth_low = split(depth)
        depth_w[n, 0:NZ, :] = depth_high
        depth_w[n, NZ:2 * NZ, :] = depth_low
        next_x = jnp.where(wide == n_wide - 1, F32(0.0), frac_x)
        next_y = jnp.where(narrow == n_narrow - 1, F32(0.0), frac_y)
        gap_8 = lax.broadcasted_iota(jnp.int32, (8, CHUNK), 0)
        weight_y = jnp.where(gap_8 == cell_y, 1.0 - frac_y, jnp.where(gap_8 == cell_y + 1, frac_y, F32(0.0)))
        weight_x = jnp.where(gap_8 == cell_x, 1.0 - frac_x, jnp.where(gap_8 == cell_x + 1, frac_x, F32(0.0)))
        last_x = jnp.where(cell_x == 7, next_x, F32(0.0))
        last_y = jnp.where(cell_y == 7, next_y, F32(0.0))
        tiles = [weight_x * last_y]
        for x in range(8):
            tiles.append(weight_x[x:x + 1] * weight_y)
        tiles.append(last_x * weight_y)
        corner = jnp.where(gap_8 == 0, weight_x[7:8], jnp.where(gap_8 == 1, last_x, F32(0.0))) * last_y
        tiles.append(corner)
        weight = jnp.concatenate(tiles, axis=0)
        plane_w[n] = weight
        lhs = [weight * (0.25 * mult[c, pl.ds(s, 1), lanes]) for c in range(3)]
        lhs.append(jnp.zeros((8, CHUNK), F32))
        acc[...] += add_spread(jnp.concatenate(lhs, axis=0), depth_w[n])
        return carry

    def part(h, carry):
        lax.fori_loop(0, CHUNKS // 2, lambda k, none: setup(h * (CHUNKS // 2) + k, none), 0, unroll=8)

        @pl.when(h == 0)
        def meet():
            pl.semaphore_wait(barrier, across * along - 1)
            start(halo_copies(0))

        return carry

    lax.fori_loop(0, 2, part, 0)
    def send_force(turn):
        for c in range(3):
            base = c * ROWS
            for t in range(11):
                part = acc[base + 8 * t:base + 8 * t + 8, :]
                if 1 <= t <= 8:
                    part = part + force[c, 8 * t - 8:8 * t, :]
                grid[turn, c, 8 * t:8 * t + 8, :] = part
        for s, tiles, extra in (
            (5, (pl.ds(8, 8, stride=8), pl.ds(9, 8, stride=8)), (72, 73)),
            (3, (pl.ds(15, 8, stride=8), pl.ds(0, 8)), (79, 81)),
        ):
            for c in range(3):
                for j in range(2):
                    grid_pack[turn, s, 16 * c + 8 * j:16 * c + 8 * j + 8, :] = grid[turn, c, tiles[j], :]
                    at = 48 + 2 * c + j
                    grid_pack[turn, s, at:at + 1, :] = grid[turn, c, extra[j]:extra[j] + 1, :]
        for c in range(3):
            for s in (0, 2, 6, 8):
                dx, dy = s // 3 - 1, s % 3 - 1
                first = 8 if dx == 1 else 64
                for j in range(2):
                    if dy == 1:
                        rows = grid[turn, c, pl.ds(first + j, 2, stride=8), :]
                    elif j == 0:
                        rows = grid[turn, c, pl.ds(first + 7, 2, stride=8), :]
                    else:
                        at = 0 if dx == 1 else 80
                        rows = grid[turn, c, at:at + 2, :]
                    grid_diag[turn, s, 4 * c + 2 * j:4 * c + 2 * j + 2, :] = rows
        for s, first, extra in ((7, 8, 0), (1, 64, 80)):
            for c in range(3):
                grid_pack[turn, s, 16 * c:16 * c + 16, :] = grid[turn, c, first:first + 16, :]
                grid_pack[turn, s, 48 + 2 * c:50 + 2 * c, :] = grid[turn, c, extra:extra + 2, :]
        start(force_copies(turn))

    send_force(0)

    def shares(n, carry):
        pad = jnp.zeros((8, CHUNK), F32)
        for s in range(SPH):
            lhs = jnp.concatenate([plane_w[s * PER_SPHERE + n], pad], axis=0)
            share_acc[s] += add_spread(lhs, depth_w[s * PER_SPHERE + n])
        return carry

    lax.fori_loop(0, PER_SPHERE, shares, 0, unroll=4)
    for s in range(SPH):
        share[s] = share_acc[s, 0:ROWS, :] * F32(1.0 / MARK)

    rhs[0:2] = jnp.zeros((2, 3, EXT, NZ), F32)
    stack[...] = jnp.zeros_like(stack)
    normal8[...] = jnp.zeros_like(normal8)
    normal8[0:3, :] = normal[...]
    normal8[4:7, :] = normal[...]

    sphere_row = lax.broadcasted_iota(jnp.int32, (8, 32), 0) // 4
    pair_s = pair_sphere[...].reshape(1, 32)
    pair_q = pair_partner[...].reshape(1, 32)
    contact_mid[...] = contact[...].reshape(1, 32)
    pair_gap = gap[...].reshape(1, 32)

    halos = halo_copies(0)
    arrive(halos)
    unpack_halo(0)
    row_id = lax.broadcasted_iota(jnp.int32, (16, NZ), 0)
    lane_id = lax.broadcasted_iota(jnp.int32, (16, NZ), 1)
    y_id = narrow * CY + jnp.where(row_id > 11, row_id - 16, row_id)

    def in_y(y):
        return (y >= 0) & (y < n_narrow * CY)

    def coefficients(i, carry):
        def viscosity(shift):
            x = wide * CX + i - 1 + shift
            inside = in_y(y_id) & (x >= 0) & (x < n_wide * CX)
            at = pl.multiple_of((i + 1 + shift) * 16, 16)
            return jnp.where(inside, ext[0, 3, pl.ds(at, 16), :], F32(0.0))

        mid = viscosity(0)
        x = wide * CX + i - 1
        around = [
            viscosity(-1),
            viscosity(1),
            jnp.where(in_y(y_id - 1), pltpu.roll(mid, 1, 0), F32(0.0)),
            jnp.where(in_y(y_id + 1), pltpu.roll(mid, 15, 0), F32(0.0)),
            jnp.where(lane_id == 0, F32(0.0), pltpu.roll(mid, 1, 1)),
            jnp.where(lane_id == NZ - 1, F32(0.0), pltpu.roll(mid, NZ - 1, 1)),
        ]
        valid = [
            (x - 1 >= 0) & (lane_id >= 0),
            (x + 1 < n_wide * CX) & (lane_id >= 0),
            in_y(y_id - 1),
            in_y(y_id + 1),
            lane_id > 0,
            lane_id < NZ - 1,
        ]
        faces = [0.5 * (mid + other) for other in around]
        diagonal = 1.0 + faces[0] + faces[1] + faces[2] + faces[3] + faces[4] + faces[5]
        inside = in_y(y_id) & (x >= 0) & (x < n_wide * CX)
        inverse = jnp.where(inside, 1.0 / diagonal, F32(0.0))
        at = pl.ds(pl.multiple_of(i * 16, 16), 16)
        for a in range(6):
            coef[a, at, :] = jnp.where(valid[a], faces[a] * inverse, F32(0.0))
        coef[6, at, :] = inverse
        return carry

    lax.fori_loop(0, 11, coefficients, 0, unroll=True)
    def own_force(turn):
        for c in range(3):
            for x in range(9):
                rhs[turn, c, pl.ds(row(x, 0), 8), :] = grid[turn, c, 8 + 8 * x:16 + 8 * x, :]
            rhs[turn, c, pl.ds(row(0, 8), 8, stride=16), :] = grid[turn, c, 0:8, :]
            rhs[turn, c, pl.ds(row(8, 8), 1), :] = grid[turn, c, 81:82, :]

    def gather_force(turn):
        def add(c, x, y, n, stride, s, value):
            at = pl.ds(row(x, y), n, stride=stride) if stride != 1 else pl.ds(row(x, y), n)
            rhs[turn, c, at, :] += received(s, value)

        copies = dict(zip(OTHERS, force_copies(turn)))
        for s in (7, 1, 5, 3, 0, 2, 6, 8):
            @pl.when(exists(s))
            def go(copy=copies[s]):
                copy.wait_recv()
            x = 8 if s // 3 == 2 else -1
            y = 8 if s % 3 == 2 else -1
            for c in range(3):
                if s in (1, 3, 5, 7):
                    tile = [grid_in[turn, s, 16 * c + 8 * j:16 * c + 8 * j + 8, :] for j in range(2)]
                    extra = grid_in[turn, s, 48 + 2 * c:50 + 2 * c, :]
                if s in (1, 7):
                    add(c, x, 0, 8, 1, s, tile[0])
                    add(c, x + 1, 0, 8, 1, s, tile[1])
                    add(c, x, 8, 2, 16, s, extra)
                elif s in (3, 5):
                    for j in range(2):
                        add(c, 0, y + j, 8, 16, s, tile[j])
                        add(c, 8, y + j, 1, 1, s, extra[j:j + 1])
                else:
                    for j in range(2):
                        at = 4 * c + 2 * j
                        add(c, x, y + j, 2, 16, s, diag_in[turn, s, at:at + 2, :])

    def neighbours(source, c, i, factors):
        def load(shift):
            return source[c, pl.ds(pl.multiple_of((i + 1 + shift) * 16, 16), 16), :]

        mid = load(0)
        value = factors[0] * load(-1) + factors[1] * load(1)
        value += factors[2] * pltpu.roll(mid, 1, 0) + factors[3] * pltpu.roll(mid, 15, 0)
        return value + (factors[4] * pltpu.roll(mid, 1, 1) + factors[5] * pltpu.roll(mid, NZ - 1, 1))

    def tiles(i):
        return pl.ds(pl.multiple_of(i * 16, 16), 16), pl.ds(pl.multiple_of((i + 1) * 16, 16), 16)

    def first_sweep(source, target):
        def one(i, carry):
            at, to = tiles(i)
            factors = [coef[a, at, :] for a in range(6)]
            for c in range(3):
                target[c, to, :] = neighbours(source, c, i, factors)
            return carry

        lax.fori_loop(0, 11, one, 0, unroll=True)

    def add_force(target, turn):
        def one(i, carry):
            at, to = tiles(i)
            inverse = coef[6, at, :]
            for c in range(3):
                value = inverse * rhs[turn, c, to, :]
                rhs[turn, c, to, :] = value
                target[c, to, :] += value
            return carry

        lax.fori_loop(0, 11, one, 0, unroll=True)

    def second_sweep(source, target, turn):
        def one(i, carry):
            at, to = tiles(i)
            factors = [coef[a, at, :] for a in range(6)]
            for c in range(3):
                target[c, to, :] = rhs[turn, c, to, :] + neighbours(source, c, i, factors)
            return carry

        lax.fori_loop(1, 10, one, 0, unroll=True)

    quarter = pair_q // 2

    def new_contact(partner, own_tile):
        closing8 = jnp.where(sphere_row == pair_q - 2 * quarter, partner, F32(0.0)) - jnp.where(
            sphere_row == pair_s, own_tile, F32(0.0)
        )
        closing = jnp.sum(normal8[...] * closing8, axis=0, keepdims=True)
        return jnp.maximum(F32(0.0), contact_mid[...] - 0.5 * (pair_gap + closing))

    def first_contact():
        partner = jnp.zeros((8, 32), F32)
        for q in range(9):
            tile = rigid[0, :, 0:32] if q == 4 else received(q, rigid_in[q, :, 0:32])
            partner = jnp.where(quarter == q, tile, partner)
        return new_contact(partner, rigid[0, :, 0:32])

    row8 = lax.broadcasted_iota(jnp.int32, (8, NZ), 0)
    lane8 = lax.broadcasted_iota(jnp.int32, (8, NZ), 1)

    def make_reach():
        for t in range(SPH):
            for x in range(9):
                spot_w[t, pl.ds(row(x, 0), 8), :] = share[t, 8 + 8 * x:16 + 8 * x, :]
            spot_w[t, pl.ds(row(0, 8), 8, stride=16), :] = share[t, 0:8, :]
            spot_w[t, pl.ds(row(8, 8), 1), :] = share[t, 81:82, :]
        for t in range(SPH):
            for i in range(11):
                to = pl.ds((i + 1) * 16, 16)
                mid = spot_w[t, to, :]
                value = jnp.zeros((16, NZ), F32)
                if i < 10:
                    value += coef[0, pl.ds((i + 1) * 16, 16), :] * spot_w[t, pl.ds((i + 2) * 16, 16), :]
                if i > 0:
                    value += coef[1, pl.ds((i - 1) * 16, 16), :] * spot_w[t, pl.ds(i * 16, 16), :]
                if 0 < i < 10:
                    at = pl.ds(i * 16, 16)
                    value += pltpu.roll(coef[2, at, :] * mid, 15, 0) + pltpu.roll(coef[3, at, :] * mid, 1, 0)
                    value += pltpu.roll(coef[4, at, :] * mid, NZ - 1, 1) + pltpu.roll(coef[5, at, :] * mid, 1, 1)
                once[t, to, :] = value
                reach[t, to, :] = coef[6, pl.ds(i * 16, 16), :] * (mid + value)
        for s in OTHERS:
            x = 8 if s // 3 == 2 else -1
            y = 8 if s % 3 == 2 else -1
            for t in range(SPH):
                for j in range(2):
                    if s in (1, 7):
                        reach_pack[s, 16 * t + 8 * j:16 * t + 8 * j + 8, :] = reach[t, pl.ds(row(x + j, 0), 8), :]
                    elif s in (3, 5):
                        reach_pack[s, 16 * t + 8 * j:16 * t + 8 * j + 8, :] = reach[t, pl.ds(row(0, y + j), 8, stride=16), :]
                        at = 32 + 2 * t + j
                        reach_pack[s, at:at + 1, :] = reach[t, pl.ds(row(8, y + j), 1), :]
                    else:
                        at = 4 * t + 2 * j
                        reach_pack[s, at:at + 2, :] = reach[t, pl.ds(row(x, y + j), 2, stride=16), :]
                if s in (1, 7):
                    reach_pack[s, 32 + 2 * t:34 + 2 * t, :] = reach[t, pl.ds(row(x, 8), 2, stride=16), :]

    def column(parts):
        tile = jnp.zeros((8, NZ), F32)
        for (t, c), part in parts.items():
            tile = jnp.where(row8 == 4 * t + c, jnp.sum(part, axis=0, keepdims=True), tile)
        return jnp.sum(tile, axis=1, keepdims=True)

    def given(turn):
        table = jnp.zeros((8, NZ), F32)
        for d in OTHERS:
            s = 8 - d
            parts = {}
            for t in range(SPH):
                for c in range(3):
                    if d in (0, 2, 6, 8):
                        part = reach_in[d, 4 * t:4 * t + 4, :] * grid_diag[turn, s, 4 * c:4 * c + 4, :]
                    else:
                        part = reach_in[d, 16 * t:16 * t + 8, :] * grid_pack[turn, s, 16 * c:16 * c + 8, :]
                        part += reach_in[d, 16 * t + 8:16 * t + 16, :] * grid_pack[turn, s, 16 * c + 8:16 * c + 16, :]
                        extra = reach_in[d, 32 + 2 * t:34 + 2 * t, :] * grid_pack[turn, s, 48 + 2 * c:50 + 2 * c, :]
                        part = jnp.concatenate([part, extra], axis=0)
                    parts[t, c] = part
            table = jnp.where(lane8 == d, received(d, column(parts)), table)
        return table

    def kept(turn, middle):
        parts = {}
        for t in range(SPH):
            for c in range(3):
                total = jnp.zeros((16, NZ), F32)
                for i in range(11):
                    at = pl.ds((i + 1) * 16, 16)
                    total += reach[t, at, :] * rhs[turn, c, at, :] + once[t, at, :] * middle[c, at, :]
                parts[t, c] = total
        return column(parts)

    def last_contact():
        lane_x, lane_y = lane8 // 3 - 1, lane8 - (lane8 // 3) * 3 - 1
        means = table8[...]
        for x, y in FAR + [(0, 0)]:
            n = (x + 2) * 5 + y + 2
            near = (lane8 < 9) & (abs(lane_x - x) <= 1) & (abs(lane_y - y) <= 1)
            if (x, y) == (0, 0):
                continue
            shifted = pltpu.roll(table_in[n], (3 * x + y) % NZ, 1)
            means += jnp.where(near & there(x, y), shifted, F32(0.0))
        partner = jnp.zeros((8, 32), F32)
        for q in range(9):
            partner = jnp.where(quarter == q, means[:, q:q + 1], partner)
        return new_contact(partner, rigid[1, :, 0:32])

    for turn in range(ITERS):
        last = turn == ITERS - 1
        if turn > 0:
            arrive(halo_copies(turn))
            unpack_halo(turn)
        own_force(turn)
        middle, done = ext.at[2], ext.at[3]
        first_sweep(ext.at[turn], middle)
        if turn > 0:
            mean_kept = kept(turn, middle)
            arrive(rigid_copies())
            contact_mid[...] = first_contact()
        push = jnp.where(sphere_row == pair_s, normal8[...] * contact_mid[...], F32(0.0))
        push_sum = 0.5 * jnp.sum(push, axis=1, keepdims=True)
        if last:
            table8[...] = jnp.where(lane8 == 4, mean_kept + push_sum, table8[...])
            for (x, y), copy in zip(FAR, shift_copies()):
                @pl.when(there(-x, -y))
                def go(copy=copy):
                    copy.start()
            for turn_before in range(ITERS):
                leave(halo_copies(turn_before))
            leave(force_copies(0))
            leave(rigid_copies())
            leave(reach_copies())
        else:
            make_reach()
            start(reach_copies())
        gather_force(turn)
        add_force(middle, turn)
        second_sweep(middle, done, turn)
        for c in range(3):
            for x in range(9):
                tile = done[c, pl.ds(row(x, 0), 8), :]
                stack[c * ROWS + 8 + 8 * x:c * ROWS + 16 + 8 * x, :] = tile
                if x < 8:
                    if last:
                        vel_out[c, 8 * x:8 * x + 8, :] = tile
                    else:
                        own[turn + 1, c, 8 * x:8 * x + 8, :] = tile
                        ext[turn + 1, c, pl.ds(row(x, 0), 8), :] = tile
            stack[c * ROWS:c * ROWS + 8, :] = done[c, pl.ds(row(0, 8), 8, stride=16), :]
            stack[c * ROWS + 81:c * ROWS + 82, :] = done[c, pl.ds(row(8, 8), 1), :]
        sums = jnp.zeros((8, NZ), F32)
        for s in range(SPH):
            for c in range(3):
                part = jnp.sum(share[s] * stack[c * ROWS:(c + 1) * ROWS, :], axis=0, keepdims=True)
                sums = jnp.where(row8 == 4 * s + c, part, sums)
        speed = jnp.sum(sums, axis=1, keepdims=True) + push_sum
        rigid[turn] = jnp.broadcast_to(speed, (8, NZ))
        if not last:
            pack_halo(turn + 1)
            start(halo_copies(turn + 1))
            start(rigid_copies())
        high, low = split(stack[...])
        left[0:PAD, 0:NZ] = high
        left[0:PAD, NZ:2 * NZ] = high
        left[PAD:2 * PAD, 0:NZ] = low
        left[PAD:2 * PAD, NZ:2 * NZ] = low
        if not last:
            acc[...] = jnp.zeros_like(acc)
        source = mult if turn == 0 else mult_mid

        def markers(n, carry):
            s, k = n // PER_SPHERE, n % PER_SPHERE
            lanes = pl.ds(pl.multiple_of(k * CHUNK, CHUNK), CHUNK)
            weight = plane_w[n]
            sampled = jnp.dot(left[0:PAD], depth_w[n], preferred_element_type=F32) + jnp.dot(left[PAD:2 * PAD, 0:NZ], depth_w[n, 0:NZ], preferred_element_type=F32)
            lhs = []
            for c in range(3):
                rows = slice(c * ROWS, (c + 1) * ROWS)
                low_rows = slice(PAD + c * ROWS, PAD + (c + 1) * ROWS)
                read = jnp.sum(sampled[rows] * weight, axis=0, keepdims=True)
                speed = rigid[turn, pl.ds(4 * s + c, 1), 0:1]
                new = source[c, pl.ds(s, 1), lanes] + 0.5 * (speed - read)
                if last:
                    mult_out[c, pl.ds(s, 1), lanes] = new
                else:
                    mult_mid[c, pl.ds(s, 1), lanes] = new
                    lhs.append(weight * (0.25 * new))
            if not last:
                lhs.append(jnp.zeros((8, CHUNK), F32))
                acc[...] += add_spread(jnp.concatenate(lhs, axis=0), depth_w[n])
            return carry

        lax.fori_loop(0, CHUNKS, markers, 0, unroll=8)
        if not last:
            send_force(turn + 1)
            arrive(reach_copies())
            table8[...] = given(turn + 1)
    leave(force_copies(ITERS - 1))
    for (x, y), copy in zip(FAR, shift_copies()):
        @pl.when(there(x, y))
        def come(copy=copy):
            copy.wait_recv()

        @pl.when(there(-x, -y))
        def gone(copy=copy):
            copy.wait_send()
    contact_out[...] = last_contact().reshape(32)


def hand_over(vel, mult, contact, vel_out, mult_out, contact_out, sem):
    copies = [
        pltpu.make_async_copy(src, dst, sem.at[k])
        for k, (src, dst) in enumerate(((vel, vel_out), (mult, mult_out), (contact, contact_out)))
    ]
    for copy in copies:
        copy.start()
    for copy in copies:
        copy.wait()


def local(
    velocity, force, visc_class, visc_table, multiplier, marker_cell, marker_frac,
    pair_sphere, pair_partner, pair_normal, pair_gap, contact_force,
):
    comps = 3
    vmem = pl.BlockSpec(memory_space=pltpu.VMEM)
    hbm = pl.BlockSpec(memory_space=pltpu.MemorySpace.HBM)
    out_shape = (
        jax.ShapeDtypeStruct((comps, CX * CY, NZ), F32),
        jax.ShapeDtypeStruct(multiplier.shape, F32),
        jax.ShapeDtypeStruct(contact_force.shape, F32),
    )
    out = pl.pallas_call(
        body,
        out_shape=tuple(pltpu.VMEM(shape.shape, shape.dtype) for shape in out_shape),
        in_specs=[hbm] * 12,
        out_specs=(vmem, vmem, vmem),
        scratch_shapes=[
            pltpu.VMEM((2, 4, CX * CY, NZ), F32),
            pltpu.VMEM((4, 4, EXT, NZ), F32),
            pltpu.VMEM((2, 2, 4, 24, NZ), F32),
            pltpu.VMEM((2, 9, 4, 24, NZ), F32),
            pltpu.VMEM((2, 9, 40, NZ), F32),
            pltpu.VMEM((2, 9, 40, NZ), F32),
            pltpu.VMEM((7, 11 * 16, NZ), F32),
            pltpu.VMEM((3, comps, EXT, NZ), F32),
            pltpu.VMEM((3, comps, ROWS, NZ), F32),
            pltpu.VMEM((2, 9, 56, NZ), F32),
            pltpu.VMEM((2, 9, 16, NZ), F32),
            pltpu.VMEM((2, 9, 56, NZ), F32),
            pltpu.VMEM((2, 9, 16, NZ), F32),
            pltpu.VMEM((CX * CY, NZ), jnp.int32),
            pltpu.SMEM(visc_table.shape, F32),
            pltpu.VMEM(marker_cell.shape, jnp.int32),
            pltpu.VMEM(marker_frac.shape, F32),
            pltpu.VMEM(multiplier.shape, F32),
            pltpu.VMEM((comps, CX * CY, NZ), F32),
            pltpu.VMEM(pair_sphere.shape, jnp.int32),
            pltpu.VMEM(pair_partner.shape, jnp.int32),
            pltpu.VMEM(pair_normal.shape, F32),
            pltpu.VMEM(pair_gap.shape, F32),
            pltpu.VMEM(contact_force.shape, F32),
            pltpu.VMEM((PAD, NZ), F32),
            pltpu.VMEM((SPH, 96, NZ), F32),
            pltpu.VMEM((SPH, ROWS, NZ), F32),
            pltpu.VMEM((CHUNKS, ROWS, CHUNK), F32),
            pltpu.VMEM((CHUNKS, 2 * NZ, CHUNK), BF16),
            pltpu.VMEM((PAD, NZ), F32),
            pltpu.VMEM((2 * PAD, 2 * NZ), BF16),
            pltpu.VMEM((comps, SPH, MARK), F32),
            pltpu.VMEM((2, 8, NZ), F32),
            pltpu.VMEM((9, 8, NZ), F32),
            pltpu.VMEM((8, 32), F32),
            pltpu.VMEM((1, 32), F32),
            pltpu.VMEM((SPH, EXT, NZ), F32),
            pltpu.VMEM((SPH, EXT, NZ), F32),
            pltpu.VMEM((SPH + 1, EXT, NZ), F32),
            pltpu.VMEM((9, 40, NZ), F32),
            pltpu.VMEM((9, 40, NZ), F32),
            pltpu.VMEM((8, NZ), F32),
            pltpu.VMEM((25, 8, NZ), F32),
            pltpu.SemaphoreType.DMA((12,)),
            pltpu.SemaphoreType.DMA((6, 9)),
            pltpu.SemaphoreType.DMA((6, 9)),
            pltpu.SemaphoreType.DMA((25,)),
            pltpu.SemaphoreType.DMA((25,)),
        ],
        compiler_params=pltpu.CompilerParams(
            collective_id=0, has_side_effects=True, vmem_limit_bytes=62 * 1024 * 1024
        ),
    )(
        velocity.reshape(comps, CX * CY, NZ), force.reshape(comps, CX * CY, NZ), visc_class.reshape(CX * CY, NZ),
        visc_table, multiplier, marker_cell, marker_frac, pair_sphere, pair_partner, pair_normal, pair_gap, contact_force,
    )
    out = pl.pallas_call(
        hand_over,
        out_shape=out_shape,
        in_specs=[vmem] * 3,
        out_specs=(hbm, hbm, hbm),
        scratch_shapes=[pltpu.SemaphoreType.DMA((3,))],
        compiler_params=pltpu.CompilerParams(vmem_limit_bytes=1024 * 1024),
    )(*out)
    return (out[0].reshape(comps, CX, CY, NZ), out[1], out[2])


def solution(mesh):
    in_specs = (
        P(None, "wide", "narrow", None),
        P(None, "wide", "narrow", None),
        P("wide", "narrow", None),
        P(),
        P(None, ("wide", "narrow"), None),
        P(("wide", "narrow"), None),
        P(None, ("wide", "narrow"), None),
        P(("wide", "narrow")),
        P(("wide", "narrow")),
        P(None, ("wide", "narrow")),
        P(("wide", "narrow")),
        P(("wide", "narrow")),
    )
    out_specs = (
        P(None, "wide", "narrow", None),
        P(None, ("wide", "narrow"), None),
        P(("wide", "narrow")),
    )
    return jax.shard_map(local, mesh=mesh, in_specs=in_specs, out_specs=out_specs, check_vma=False)
```
